32 devices in a mesh: comm: 16 (over z, x, core), blk: 2 (over y).
Axes of the slice: x: 2, y: 2, z: 4, core: 2. Of those that a mesh axis runs over, the one named last changes fastest.
Arguments:
- features: float32 [4096, 256], P(('comm', 'blk')), may hold values from -6 to 6
- tiles: float32 [4096, 256], P(('comm', 'blk')), may hold values from -0.375 to 0.375
- weight: float32 [256, 256], replicated, may hold values from -0.375 to 0.375
- cotangent: float32 [4096, 256], P(('comm', 'blk')), may hold values from -6 to 6
- send_count: int32 [32, 16], P(('comm', 'blk')), may hold values from 0 to 16, as said below
- send_index: int32 [32, 256], P(('comm', 'blk')), may hold values from 0 to 127
- cross_dst: int32 [32, 256], P(('comm', 'blk')), may hold values from 0 to 127
- cross_weight: float32 [32, 256], P(('comm', 'blk')), may hold values from -2.4 to 2.4
Outputs:
- output: float32 [4096, 256], P(('comm', 'blk'))
- grad_features: float32 [4096, 256], P(('comm', 'blk'))
- grad_weight: float32 [256, 256], replicated
The draws below stay inside these ranges and needn't reach their ends.
Inputs may be any that keep to these rules, and one draw needn't show every extreme that they name: send_count[d, p] is 0 where p is d's own community and at least 1 elsewhere; every device sends exactly 16 rows to some other community.
All inputs are finite; a program needn't handle non-finite values.
Results may differ from the reference program's by a relative error of at most 0.0003.
Values sent between devices are 32-bit elements; how exact they have to be, the bound alone decides.
No kernel may reach another device: no remote copies, remote signals or barrier semaphores. Data moves between devices by JAX's collectives and lax.ppermute only.
A program may use at most 64 MiB of HBM per device.

```python
import jax
import jax.numpy as jnp
from jax import lax

ROWS = 128
H = 256
CAP = 16
NODES = 4096
BLOCK_COLS = 256
SLOTS = 256
N_COMM = 16
N_BLK = 2


def draw_send_count(key, part):
    key = jax.random.fold_in(key, 11)
    first, second = jax.random.split(key)
    senders = N_COMM * N_BLK
    counts = jax.random.randint(first, (senders, N_COMM), 1, CAP + 1)
    group = jnp.arange(senders, dtype=jnp.int32) // N_BLK
    full_peer = (group + 1 + jax.random.randint(second, (senders,), 0, N_COMM - 1)) % N_COMM
    peers = jnp.arange(N_COMM, dtype=jnp.int32)
    counts = jnp.where(peers[None, :] == full_peer[:, None], CAP, counts)
    counts = jnp.where(peers[None, :] == group[:, None], 0, counts)
    return counts.astype(jnp.int32)


def place_ends(entries, key, low, high):
    longest = entries.shape.index(max(entries.shape))
    spots = []
    for shift in (0, 1):
        where = [jax.random.randint(jax.random.fold_in(key, axis), (), 0, length) for axis, length in enumerate(entries.shape)]
        where[longest] = (where[longest] + shift) % entries.shape[longest]
        spots.append(tuple(where))
    return entries.at[spots[0]].set(low).at[spots[1]].set(high)


def steps_of(rng, extent, cuts, smallest, top_value):
    def one(dim, parts):
        heights = jax.random.uniform(jax.random.fold_in(jax.random.fold_in(rng, 6), dim), (parts,), jnp.float32, smallest / len(cuts), top_value / len(cuts))
        return jnp.repeat(jnp.exp(heights), extent[dim] // parts).reshape((-1,) + (1,) * (len(extent) - dim - 1))

    gain = one(*cuts[0])
    for cut in cuts[1:]:
        gain = gain * one(*cut)
    return gain


def gaussian(own_key, dims, deviation, bound, pieces=(), held_as=jnp.bfloat16):
    level = steps_of(own_key, dims, pieces, -0.22, 0.18) if pieces else 1.0
    values = jax.random.normal(own_key, dims, jnp.float32) * deviation * level
    return jnp.minimum(jnp.maximum(values, -bound), bound).astype(held_as)


def setup_inputs(seed: int = 0) -> dict:
    streams_of = jax.random.split(jax.random.key(seed), 9)
    features = gaussian(streams_of[0], (NODES, H), 1.0, 6.0, ((0, 32),), jnp.float32)
    tiles = gaussian(streams_of[1], (NODES, BLOCK_COLS), BLOCK_COLS ** -0.5, 0.375, ((0, 32),), jnp.float32)
    weight = gaussian(streams_of[2], (H, H), H ** -0.5, 0.375, (), jnp.float32)
    cotangent = gaussian(streams_of[3], (NODES, H), 1.0, 6.0, ((0, 32),), jnp.float32)
    send_count = draw_send_count(jax.random.fold_in(streams_of[8], 71), 0)
    send_index = place_ends(jax.random.randint(streams_of[5], (N_COMM * N_BLK, SLOTS), 0, ROWS), jax.random.fold_in(streams_of[5], 1), 0, ROWS - 1).astype(jnp.int32)
    cross_dst = place_ends(jax.random.randint(streams_of[6], (N_COMM * N_BLK, SLOTS), 0, ROWS), jax.random.fold_in(streams_of[6], 1), 0, ROWS - 1).astype(jnp.int32)
    cross_weight = gaussian(streams_of[7], (N_COMM * N_BLK, SLOTS), 0.4, 2.4, ((0, 32),), jnp.float32)
    return {"features": features, "tiles": tiles, "weight": weight, "cotangent": cotangent, "send_count": send_count, "send_index": send_index, "cross_dst": cross_dst, "cross_weight": cross_weight}


def forward(features, weight, tiles, send_count, send_index, cross_dst, cross_weight):
    groups = N_COMM
    blocks = N_BLK
    grid = features.reshape(groups, blocks, ROWS, H)
    flat = features.reshape(groups, blocks * ROWS, H)
    tile_grid = tiles.reshape(groups, blocks, ROWS, blocks * ROWS)
    index = send_index.reshape(groups, blocks, groups, CAP)
    count = send_count.reshape(groups, blocks, groups)
    targets = cross_dst.reshape(groups, blocks, groups * CAP)
    edge_weight = cross_weight.reshape(groups, blocks, groups * CAP)
    slots = jnp.arange(CAP, dtype=jnp.int32)

    def one_group(group):
        local = jnp.einsum('brk,kh->brh', tile_grid[group], flat[group], precision=lax.Precision.HIGHEST)
        rows_in = index[:, :, group, :]
        picked = jax.vmap(jax.vmap(lambda table, where: table[where]))(grid, rows_in)
        valid = (slots[None, None, :] < count[:, :, group][:, :, None]).astype(jnp.float32)
        picked = picked * valid[:, :, :, None]
        received = jnp.transpose(picked, (1, 0, 2, 3)).reshape(blocks, groups * CAP, H)
        terms = edge_weight[group][:, :, None] * received
        cross = jax.vmap(lambda term, dest: jax.ops.segment_sum(term, dest, num_segments=ROWS))(terms, targets[group])
        return local + cross
    aggregated = lax.map(one_group, jnp.arange(groups, dtype=jnp.int32)).reshape(NODES, H)
    pre = jnp.dot(aggregated, weight, precision=lax.Precision.HIGHEST)
    return jax.nn.gelu(pre, approximate=False)

def reference(features, tiles, weight, cotangent, send_count, send_index, cross_dst, cross_weight):

    def layer(feature_in, weight_in):
        return forward(feature_in, weight_in, tiles, send_count, send_index, cross_dst, cross_weight)
    output, pull = jax.vjp(layer, features, weight)
    grad_features, grad_weight = pull(cotangent)
    return (output, grad_features, grad_weight * NODES ** (-0.5))
```

```python
import functools
import math

import jax
import jax.numpy as jnp
from jax import lax
from jax.experimental import pallas as pl
from jax.experimental.pallas import tpu as pltpu
from jax.sharding import PartitionSpec as P

F32 = jnp.float32
BF16 = jnp.bfloat16
VMEM = pl.BlockSpec(memory_space=pltpu.VMEM)
HBM = pl.BlockSpec(memory_space=pltpu.HBM)


def split(value):
    high = value.astype(BF16)
    return high, (value - high.astype(F32)).astype(BF16)


def product(a, b, dims):
    return lax.dot_general(a, b, (dims, ((), ())), preferred_element_type=F32)


def dot3(a, b, dims=((1,), (0,))):
    (a_high, a_low), (b_high, b_low) = a, b
    return (product(a_low, b_high, dims) + product(a_high, b_low, dims)) + product(a_high, b_high, dims)


def dot_onehot(a, b, dims):
    return product(a, b[1], dims) + product(a, b[0], dims)


def tree(terms):
    while len(terms) > 1:
        terms = [terms[i] + terms[i + 1] for i in range(0, len(terms), 2)]
    return terms[0]


def send_matrix(counts, index, rows):
    groups, slots = counts.shape[1], index.shape[1]
    per_peer = slots // groups
    lane = lax.broadcasted_iota(jnp.int32, (groups, slots), 1)
    first = lax.broadcasted_iota(jnp.int32, (groups, slots), 0) * per_peer
    of_peer = ((lane >= first) & (lane < first + per_peer)).astype(F32)
    limit = jnp.dot(counts.astype(F32), of_peer, preferred_element_type=F32)
    place = lax.broadcasted_iota(jnp.int32, (1, slots), 1) % per_peer
    chosen = jnp.where(place.astype(F32) < limit, index, -1)
    return (lax.broadcasted_iota(jnp.int32, (rows, slots), 0) == chosen).astype(F32).astype(BF16)


def gather_kernel(
    count_hbm, index_hbm, features_hbm, own_ref, give_ref, chosen_ref, count_ref, index_ref, features_ref, rows_ref, sems
):
    pairs = ((count_hbm, count_ref), (index_hbm, index_ref), (features_hbm, features_ref))
    copies = [pltpu.make_async_copy(source, target, sems.at[i]) for i, (source, target) in enumerate(pairs)]
    for copy in copies:
        copy.start()
    copies[0].wait()
    copies[1].wait()
    chosen = send_matrix(count_ref[...], index_ref[...], features_ref.shape[0])
    chosen_ref[...] = chosen
    copies[2].wait()
    rows_ref[...] = dot_onehot(chosen, split(features_ref[...]), ((0,), (0,)))
    me = lax.axis_index("comm")
    chips, per_peer = own_ref.shape[:2]
    for mask in range(chips):
        for k, out_ref in enumerate((own_ref, give_ref)):
            start = lax.bitwise_xor(me, 2 * mask + (k ^ (mask > 0))) * per_peer
            out_ref[mask] = rows_ref[pl.ds(pl.multiple_of(start, per_peer), per_peer), :]


def prepare_kernel(
    near_ref, far_ref, tiles_ref, weight_ref, target_ref, edge_ref,
    local_ref, cross_ref, tiles_out, weight_out,
):
    rows = near_ref.shape[0]
    blocks = far_ref.shape[0] + 1
    slots = target_ref.shape[1]
    me = lax.axis_index("blk")

    total = None
    for step in range(blocks):
        start = lax.rem(me + step, blocks) * rows
        tile = split(tiles_ref[:, pl.ds(pl.multiple_of(start, rows), rows)])
        tiles_out[step, 0], tiles_out[step, 1] = tile
        term = dot3(tile, split(near_ref[...] if step == 0 else far_ref[step - 1]))
        total = term if total is None else total + term
    local_ref[...] = total
    hit = lax.broadcasted_iota(jnp.int32, (rows, slots), 0) == target_ref[...]
    cross_ref[0], cross_ref[1] = split(jnp.where(hit, edge_ref[...], 0.0))
    weight_out[0], weight_out[1] = split(weight_ref[...])


def chunk_number(chunks):
    blocks = lax.axis_size("blk")
    number = lax.axis_index("comm") * blocks + lax.axis_index("blk")
    outer = lax.div(number, chunks)
    crossed = lax.rem(outer + lax.div(outer, 2), 2) * blocks
    return lax.bitwise_xor(lax.rem(number, chunks), crossed)


def layer_kernel(
    order, parities, local_ref, cross_ref, weight_ref, cotangent_ref, own_ref, got_ref, *refs
):
    chips, per_peer = own_ref.shape[:2]
    arrived_refs, refs = refs[: chips - 1], refs[chips - 1 :]
    out_ref, spread_ref, keep_ref, give_ref, *partial_refs, slots_ref, terms_ref = refs
    peer = lax.axis_index("comm")
    for mask in range(chips):
        for k in range(2):
            start = lax.bitwise_xor(peer, 2 * mask + (k ^ (mask > 0))) * per_peer
            block = arrived_refs[mask - 1][k] if mask else (got_ref if k else own_ref)[0]
            slots_ref[pl.ds(pl.multiple_of(start, per_peer), per_peer), :] = block
    cross = cross_ref[0], cross_ref[1]
    weight = weight_ref[0], weight_ref[1]

    aggregated = split(local_ref[...] + dot3(cross, split(slots_ref[...])))
    pre = dot3(aggregated, weight)
    cdf = 0.5 * (1.0 + lax.erf(pre * math.sqrt(0.5)))
    density = jnp.exp(-0.5 * pre * pre) * (1.0 / math.sqrt(2.0 * math.pi))
    grad_pre = split(cotangent_ref[...] * (cdf + pre * density))
    out_ref[...] = pre * cdf
    terms_ref[...] = dot3(aggregated, grad_pre, ((0,), (0,)))
    spread = split(dot3(grad_pre, weight, ((1,), (1,))))
    spread_ref[0], spread_ref[1] = spread
    slots_ref[...] = dot3(cross, spread, ((0,), (0,)))

    half = 0
    if partial_refs:
        partial_refs[0][...] = terms_ref[...]
    else:
        half = terms_ref.shape[0] // 2
        share = terms_ref.shape[0] // len(order)
        me = chunk_number(len(order))
        for place, relative in enumerate(order):
            start = lax.bitwise_xor(me, relative) * share
            chunk = terms_ref[pl.ds(pl.multiple_of(start, share), share), :]
            target_ref = keep_ref if place < len(order) // 2 else give_ref
            target_ref[pl.ds(place * share % half, share), :] = chunk
    for mask in range(chips):
        for k, target_ref in enumerate((keep_ref, give_ref)):
            start = lax.bitwise_xor(peer, 2 * mask + (k ^ parities[mask])) * per_peer
            block = slots_ref[pl.ds(pl.multiple_of(start, per_peer), per_peer), :]
            target_ref[pl.ds(half + mask * per_peer, per_peer), :] = block


def place_kernel(order, mine_ref, other_ref, out_ref):
    half, share = mine_ref.shape[:2]
    me = chunk_number(len(order))
    for i, relative in enumerate(order):
        start = lax.bitwise_xor(me, relative) * share
        out_ref[pl.ds(pl.multiple_of(start, share), share), :] = mine_ref[i] if i < half else other_ref[i - half]


def inner_kernel(tiles_ref, spread_ref, value_ref, near_ref, far_ref, out_ref):
    spread = spread_ref[0], spread_ref[1]
    for step in range(far_ref.shape[0]):
        far_ref[step] = dot3((tiles_ref[step + 1, 0], tiles_ref[step + 1, 1]), spread, ((0,), (0,)))
    near_ref[...] = dot3((tiles_ref[0, 0], tiles_ref[0, 1]), spread, ((0,), (0,)))
    out_ref[...] = value_ref[...]


def value_of(piece, refs):
    if isinstance(piece, list):
        return tree([value_of(term, refs) for term in piece])
    source, first, rows = piece
    return refs[source][first : first + rows, :]


def rows_of(piece):
    return rows_of(piece[0]) if isinstance(piece, list) else piece[2]


def leaves(piece):
    return [leaf for term in piece for leaf in leaves(term)] if isinstance(piece, list) else [piece]


def renumber(piece, used):
    if isinstance(piece, list):
        return [renumber(term, used) for term in piece]
    return (used.index(piece[0]), *piece[1:])


def pack_kernel(layout, scale, count, *refs):
    for pieces, out_ref in zip(layout, refs[count:]):
        first = 0
        for piece in pieces:
            rows = rows_of(piece)
            value = value_of(piece, refs)
            out_ref[first : first + rows, :] = value if scale is None else value * scale
            first += rows


def finish_kernel(blocks, far, chosen_ref, near_ref, *refs):
    *refs, grad_ref, slots_ref = refs
    peer = lax.axis_index("comm")
    for distance, piece in blocks:
        rows = piece[2]
        start = lax.bitwise_xor(peer, distance) * rows
        slots_ref[pl.ds(pl.multiple_of(start, rows), rows), :] = value_of(piece, refs)
    total = near_ref[...]
    for piece in far:
        total += value_of(piece, refs)
    grad_ref[...] = total + dot_onehot(chosen_ref[...], split(slots_ref[...]), ((1,), (0,)))


def kernel(body, name, out, operands, spec=VMEM, scratch=(), flops=0, traffic=0, after=()):
    count = len(operands)
    if spec is HBM:
        operands = [pltpu.with_memory_space_constraint(x, pltpu.HBM) for x in operands]
    return pl.pallas_call(
        lambda *refs: body(*refs[:count], *refs[count + len(after) :]),
        out_shape=out,
        in_specs=[spec] * count + [pl.BlockSpec(memory_space=pl.ANY)] * len(after),
        out_specs=jax.tree.map(lambda _: VMEM, out),
        scratch_shapes=list(scratch),
        compiler_params=pltpu.CompilerParams(vmem_limit_bytes=16 * 1024 * 1024),
        cost_estimate=pl.CostEstimate(flops=flops, bytes_accessed=traffic, transcendentals=0),
        name=name,
    )(*operands, *after)


def body(features, tiles, weight, cotangent, send_count, send_index, cross_dst, cross_weight):
    rows, width = features.shape
    groups = lax.axis_size("comm")
    blocks = lax.axis_size("blk")
    slots = send_index.shape[1]
    per_peer = slots // groups
    nodes = rows * groups * blocks
    array = jax.ShapeDtypeStruct
    work = 2 * rows * slots * width

    def shift(value, step):
        pairs = [(i, (i + step) % blocks) for i in range(blocks)]
        return lax.ppermute(value, "blk", pairs)

    def exchange(value):
        return lax.all_to_all(value, "comm", split_axis=0, concat_axis=0, tiled=True)

    both = ("comm", "blk")
    devices = groups * blocks
    outer = min(4, groups // 2)
    chunks = devices // outer
    share = width // chunks
    low, high = blocks.bit_length() - 1, chunks.bit_length() - 1
    others = list(range(low)) + list(range(low + 1, high))
    pairs = [others[i : i + 2] for i in range(0, len(others), 2)]

    core = 1 << low
    outer_bits = list(range(high, devices.bit_length() - 1))

    def masks(bits, straight=()):
        plain = [sum((i >> j & 1) << bit for j, bit in enumerate(bits)) for i in range(1 << len(bits))]
        if bits is outer_bits:
            return [mask ^ core * (i.bit_count() % 2) for i, mask in enumerate(plain)]
        return [mask if mask in (0, core) or mask in straight else mask ^ core for mask in plain]

    def order_of(straight=()):
        order = [0]
        for bits in reversed([[low]] + pairs):
            order = [mask ^ place for mask in masks(bits, straight) for place in order]
        return order

    straight = (1,) if blocks == 2 else ()
    order, gather_order = order_of(straight), order_of()
    way_bits = [sum(1 << bit - low - 1 for bit in bits if bit > low) for bits in pairs]
    parities = [
        (sum(bool(chip & bits) for bits in way_bits) + (chip >> high - low - 1).bit_count()) % 2
        for chip in range(groups // 2)
    ]

    def swap(value, mask):
        return lax.ppermute(value, both, [(i, i ^ mask) for i in range(devices)]) if mask else value

    far = jnp.stack([shift(features, -step) for step in range(1, blocks)])
    own, give, chosen = kernel(
        gather_kernel,
        "gather",
        (
            array((groups // 2, per_peer, width), F32),
            array((groups // 2, per_peer, width), F32),
            array((rows, slots), BF16),
        ),
        (send_count, send_index, features),
        spec=HBM,
        scratch=(
            pltpu.VMEM(send_count.shape, jnp.int32),
            pltpu.VMEM(send_index.shape, jnp.int32),
            pltpu.VMEM(features.shape, F32),
            pltpu.VMEM((slots, width), F32),
            pltpu.SemaphoreType.DMA((3,)),
        ),
        flops=work,
        traffic=4 * (rows + slots) * width,
    )
    got = swap(give, 1 << low)
    packed = jnp.stack([own, got], axis=1)
    arrived = [swap(packed[mask], 2 * mask + 1 << low) for mask in range(1, groups // 2)]
    local, cross, tile_parts, weight_parts = kernel(
        prepare_kernel,
        "prepare",
        (
            array((rows, width), F32),
            array((2, rows, slots), BF16),
            array((blocks, 2, rows, rows), BF16),
            array((2, width, width), BF16),
        ),
        (features, far, tiles, weight, cross_dst, cross_weight),
        flops=3 * work,
        traffic=4 * (4 * rows + width) * width,
    )
    aligned = share % 8 == 0
    half = width // 2
    held = array((slots // 2 + (half if aligned else 0), width), F32)
    value, spread, keep, give, *partial = kernel(
        functools.partial(layer_kernel, order, parities),
        "layer",
        (array((rows, width), F32), array((2, rows, width), BF16), held, held)
        + (() if aligned else (array((width, width), F32),)),
        (local, cross, weight_parts, cotangent, own, got, *arrived),
        scratch=(pltpu.VMEM((slots, width), F32), pltpu.VMEM((width, width), F32)),
        flops=15 * work,
        traffic=4 * (4 * rows + 2 * slots) * width,
    )
    if not aligned:
        ordered = partial[0].reshape(chunks, share, width)[chunk_number(chunks) ^ jnp.array(order)]
        keep = jnp.concatenate([ordered[: chunks // 2].reshape(half, width), keep])
        give = jnp.concatenate([ordered[chunks // 2 :].reshape(half, width), give])
    inner, leaving, output = kernel(
        inner_kernel,
        "inner",
        (array((rows, width), F32), array((blocks - 1, rows, width), F32), array((rows, width), F32)),
        (tile_parts, spread, value),
        flops=3 * work,
        traffic=4 * 6 * rows * width,
    )

    arrays = [keep, give, swap(give, 1 << low)]
    terms = [[(0, i * share, share), (2, i * share, share)] for i in range(chunks // 2)]
    moving = {
        2 * m + parities[m]: [(k, (2 * k, half + m * per_peer, per_peer)) for k in range(2)]
        for m in range(groups // 2)
    }
    far_pieces = []

    def pack(name, layout, scale=None):
        used = sorted({leaf[0] for pieces in layout for leaf in leaves(pieces)})
        layout = [[renumber(piece, used) for piece in pieces] for pieces in layout]
        out = tuple(array((sum(map(rows_of, pieces)), width), F32) for pieces in layout)
        operands = [arrays[i] for i in used]
        traffic = 8 * width * sum(o.shape[0] for o in out)
        return kernel(functools.partial(pack_kernel, layout, scale, len(used)), name, out, operands, traffic=traffic)

    for bits in pairs + [outer_bits]:
        last = bits is outer_bits
        keeps = len(terms) if last else len(terms) >> len(bits)
        layout, riders = [], []
        partners = list(enumerate(masks(bits, straight)))[:0:-1]
        for i, mask in partners:
            pieces = list(terms) if last else terms[i * keeps : (i + 1) * keeps]
            way, across = mask >> low, mask & (core - 1)
            all_ways = sum(1 << bit for bit in bits) >> low
            going = [q for q in sorted(moving) if not across and q & all_ways == way & all_ways]
            riders.append([(q, come) for q in going for come, _ in moving[q]])
            pieces += [piece for q in going for _, piece in moving[q]]
            if blocks == 2 and mask == 1:
                arrays.append(leaving[0])
                pieces.append((len(arrays) - 1, 0, rows))
            layout.append(pieces)
        sent = pack("pack", layout)
        came = []
        for (_, mask), value, rides in zip(partners, sent, riders):
            arrays.append(swap(value, mask))
            number, first = len(arrays) - 1, 0
            came.append([(number, j * share, share) for j in range(keeps)])
            first = keeps * share
            for q, come in rides:
                way = mask >> low
                moving.setdefault(q ^ way, []).append((come ^ way, (number, first, per_peer)))
                first += per_peer
            if blocks == 2 and mask == 1:
                far_pieces.append((number, first, rows))
            for q in {q for q, _ in rides}:
                del moving[q]
        terms = [[terms[j]] + [pieces[j] for pieces in reversed(came)] for j in range(keeps)]
    if blocks > 2:
        for step in range(1, blocks):
            arrays.append(shift(leaving[step - 1], step))
            far_pieces.append((len(arrays) - 1, 0, rows))

    sums = pack("sum", [terms], nodes ** (-0.5))[0].reshape(1, share, width)
    for bits in reversed(pairs):
        sums = jnp.concatenate([swap(sums, mask) for mask in masks(bits)])
    other = swap(sums, 1 << low)
    if aligned:
        grad_weight = kernel(
            functools.partial(place_kernel, gather_order),
            "place",
            array((width, width), F32),
            (sums, other),
            traffic=8 * width * width,
        )
    else:
        places = jnp.array([gather_order.index(i) for i in range(chunks)])[chunk_number(chunks) ^ jnp.arange(chunks)]
        grad_weight = jnp.concatenate([sums, other])[places].reshape(width, width)

    came = moving[0]
    used = sorted({piece[0] for _, piece in came} | {piece[0] for piece in far_pieces})
    grad_features = kernel(
        functools.partial(
            finish_kernel,
            [(distance, renumber(piece, used)) for distance, piece in came],
            [renumber(piece, used) for piece in far_pieces],
        ),
        "finish",
        array((rows, width), F32),
        (chosen, inner, *(arrays[i] for i in used)),
        scratch=(pltpu.VMEM((slots, width), F32),),
        flops=2 * work,
        traffic=4 * (3 * rows + slots) * width,
    )
    return (output, grad_features, grad_weight)


def solution(mesh):
    return jax.shard_map(
        body,
        mesh=mesh,
        in_specs=(
            P(("comm", "blk"), None),
            P(("comm", "blk"), None),
            P(),
            P(("comm", "blk"), None),
            P(("comm", "blk"), None),
            P(("comm", "blk"), None),
            P(("comm", "blk"), None),
            P(("comm", "blk"), None),
        ),
        out_specs=(P(("comm", "blk"), None), P(("comm", "blk"), None), P()),
        check_vma=False,
    )
```

```python
import functools
import math

import jax
import jax.numpy as jnp
from jax import lax
from jax.experimental import pallas as pl
from jax.experimental.pallas import tpu as pltpu
from jax.sharding import PartitionSpec as P

F32 = jnp.float32
BF16 = jnp.bfloat16
VMEM = pl.BlockSpec(memory_space=pltpu.VMEM)
HBM = pl.BlockSpec(memory_space=pltpu.HBM)


def split(value):
    high = value.astype(BF16)
    return high, (value - high.astype(F32)).astype(BF16)


def product(a, b, dims):
    return lax.dot_general(a, b, (dims, ((), ())), preferred_element_type=F32)


def dot3(a, b, dims=((1,), (0,))):
    (a_high, a_low), (b_high, b_low) = a, b
    return (product(a_low, b_high, dims) + product(a_high, b_low, dims)) + product(a_high, b_high, dims)


def dot_onehot(a, b, dims):
    return product(a, b[1], dims) + product(a, b[0], dims)


def tree(terms):
    while len(terms) > 1:
        terms = [terms[i] + terms[i + 1] for i in range(0, len(terms), 2)]
    return terms[0]


def send_matrix(counts, index, rows):
    groups, slots = counts.shape[1], index.shape[1]
    per_peer = slots // groups
    lane = lax.broadcasted_iota(jnp.int32, (groups, slots), 1)
    first = lax.broadcasted_iota(jnp.int32, (groups, slots), 0) * per_peer
    of_peer = ((lane >= first) & (lane < first + per_peer)).astype(F32)
    limit = jnp.dot(counts.astype(F32), of_peer, preferred_element_type=F32)
    place = lax.broadcasted_iota(jnp.int32, (1, slots), 1) % per_peer
    chosen = jnp.where(place.astype(F32) < limit, index, -1)
    return (lax.broadcasted_iota(jnp.int32, (rows, slots), 0) == chosen).astype(F32).astype(BF16)


def gather_kernel(
    count_hbm, index_hbm, features_hbm, own_ref, give_ref, chosen_ref, count_ref, index_ref, features_ref, rows_ref, sems
):
    pairs = ((count_hbm, count_ref), (index_hbm, index_ref), (features_hbm, features_ref))
    copies = [pltpu.make_async_copy(source, target, sems.at[i]) for i, (source, target) in enumerate(pairs)]
    for copy in copies:
        copy.start()
    copies[0].wait()
    copies[1].wait()
    chosen = send_matrix(count_ref[...], index_ref[...], features_ref.shape[0])
    chosen_ref[...] = chosen
    copies[2].wait()
    rows_ref[...] = dot_onehot(chosen, split(features_ref[...]), ((0,), (0,)))
    me = lax.axis_index("comm")
    chips, per_peer = own_ref.shape[:2]
    for mask in range(chips):
        for k, out_ref in enumerate((own_ref, give_ref)):
            start = lax.bitwise_xor(me, 2 * mask + (k ^ (mask > 0))) * per_peer
            out_ref[mask] = rows_ref[pl.ds(pl.multiple_of(start, per_peer), per_peer), :]


def prepare_kernel(
    near_ref, far_ref, tiles_ref, weight_ref, target_ref, edge_ref,
    local_ref, cross_ref, tiles_out, weight_out,
):
    rows = near_ref.shape[0]
    blocks = far_ref.shape[0] + 1
    slots = target_ref.shape[1]
    me = lax.axis_index("blk")

    total = None
    for step in range(blocks):
        start = lax.rem(me + step, blocks) * rows
        tile = split(tiles_ref[:, pl.ds(pl.multiple_of(start, rows), rows)])
        tiles_out[step, 0], tiles_out[step, 1] = tile
        term = dot3(tile, split(near_ref[...] if step == 0 else far_ref[step - 1]))
        total = term if total is None else total + term
    local_ref[...] = total
    hit = lax.broadcasted_iota(jnp.int32, (rows, slots), 0) == target_ref[...]
    cross_ref[0], cross_ref[1] = split(jnp.where(hit, edge_ref[...], 0.0))
    weight_out[0], weight_out[1] = split(weight_ref[...])


def chunk_number(chunks):
    blocks = lax.axis_size("blk")
    number = lax.axis_index("comm") * blocks + lax.axis_index("blk")
    outer = lax.div(number, chunks)
    crossed = lax.rem(outer + lax.div(outer, 2), 2) * blocks
    return lax.bitwise_xor(lax.rem(number, chunks), crossed)


def layer_kernel(
    order, parities, local_ref, cross_ref, weight_ref, cotangent_ref, own_ref, got_ref, *refs
):
    chips, per_peer = own_ref.shape[:2]
    arrived_refs, refs = refs[: chips - 1], refs[chips - 1 :]
    out_ref, spread_ref, keep_ref, give_ref, *partial_refs, slots_ref, terms_ref = refs
    peer = lax.axis_index("comm")
    for mask in range(chips):
        for k in range(2):
            start = lax.bitwise_xor(peer, 2 * mask + (k ^ (mask > 0))) * per_peer
            block = arrived_refs[mask - 1][k] if mask else (got_ref if k else own_ref)[0]
            slots_ref[pl.ds(pl.multiple_of(start, per_peer), per_peer), :] = block
    cross = cross_ref[0], cross_ref[1]
    weight = weight_ref[0], weight_ref[1]

    aggregated = split(local_ref[...] + dot3(cross, split(slots_ref[...])))
    pre = dot3(aggregated, weight)
    cdf = 0.5 * (1.0 + lax.erf(pre * math.sqrt(0.5)))
    density = jnp.exp(-0.5 * pre * pre) * (1.0 / math.sqrt(2.0 * math.pi))
    grad_pre = split(cotangent_ref[...] * (cdf + pre * density))
    out_ref[...] = pre * cdf
    terms_ref[...] = dot3(aggregated, grad_pre, ((0,), (0,)))
    spread = split(dot3(grad_pre, weight, ((1,), (1,))))
    spread_ref[0], spread_ref[1] = spread
    slots_ref[...] = dot3(cross, spread, ((0,), (0,)))

    half = 0
    if partial_refs:
        partial_refs[0][...] = terms_ref[...]
    else:
        half = terms_ref.shape[0] // 2
        share = terms_ref.shape[0] // len(order)
        me = chunk_number(len(order))
        for place, relative in enumerate(order):
            start = lax.bitwise_xor(me, relative) * share
            chunk = terms_ref[pl.ds(pl.multiple_of(start, share), share), :]
            target_ref = keep_ref if place < len(order) // 2 else give_ref
            target_ref[pl.ds(place * share % half, share), :] = chunk
    for mask in range(chips):
        for k, target_ref in enumerate((keep_ref, give_ref)):
            start = lax.bitwise_xor(peer, 2 * mask + (k ^ parities[mask])) * per_peer
            block = slots_ref[pl.ds(pl.multiple_of(start, per_peer), per_peer), :]
            target_ref[pl.ds(half + mask * per_peer, per_peer), :] = block


def place_kernel(order, mine_ref, other_ref, out_ref):
    half, share = mine_ref.shape[:2]
    me = chunk_number(len(order))
    for i, relative in enumerate(order):
        start = lax.bitwise_xor(me, relative) * share
        out_ref[pl.ds(pl.multiple_of(start, share), share), :] = mine_ref[i] if i < half else other_ref[i - half]


def inner_kernel(tiles_ref, spread_ref, value_ref, near_ref, far_ref, out_ref):
    spread = spread_ref[0], spread_ref[1]
    for step in range(far_ref.shape[0]):
        far_ref[step] = dot3((tiles_ref[step + 1, 0], tiles_ref[step + 1, 1]), spread, ((0,), (0,)))
    near_ref[...] = dot3((tiles_ref[0, 0], tiles_ref[0, 1]), spread, ((0,), (0,)))
    out_ref[...] = value_ref[...]


def value_of(piece, refs):
    if isinstance(piece, list):
        return tree([value_of(term, refs) for term in piece])
    source, first, rows = piece
    return refs[source][first : first + rows, :]


def rows_of(piece):
    return rows_of(piece[0]) if isinstance(piece, list) else piece[2]


def leaves(piece):
    return [leaf for term in piece for leaf in leaves(term)] if isinstance(piece, list) else [piece]


def renumber(piece, used):
    if isinstance(piece, list):
        return [renumber(term, used) for term in piece]
    return (used.index(piece[0]), *piece[1:])


def pack_kernel(layout, scale, count, *refs):
    for pieces, out_ref in zip(layout, refs[count:]):
        first = 0
        for piece in pieces:
            rows = rows_of(piece)
            value = value_of(piece, refs)
            out_ref[first : first + rows, :] = value if scale is None else value * scale
            first += rows


def finish_kernel(blocks, far, chosen_ref, near_ref, *refs):
    *refs, grad_ref, slots_ref = refs
    peer = lax.axis_index("comm")
    for distance, piece in blocks:
        rows = piece[2]
        start = lax.bitwise_xor(peer, distance) * rows
        slots_ref[pl.ds(pl.multiple_of(start, rows), rows), :] = value_of(piece, refs)
    total = near_ref[...]
    for piece in far:
        total += value_of(piece, refs)
    grad_ref[...] = total + dot_onehot(chosen_ref[...], split(slots_ref[...]), ((1,), (0,)))


def kernel(body, name, out, operands, spec=VMEM, scratch=(), flops=0, traffic=0, after=()):
    count = len(operands)
    if spec is HBM:
        operands = [pltpu.with_memory_space_constraint(x, pltpu.HBM) for x in operands]
    return pl.pallas_call(
        lambda *refs: body(*refs[:count], *refs[count + len(after) :]),
        out_shape=out,
        in_specs=[spec] * count + [pl.BlockSpec(memory_space=pl.ANY)] * len(after),
        out_specs=jax.tree.map(lambda _: VMEM, out),
        scratch_shapes=list(scratch),
        compiler_params=pltpu.CompilerParams(vmem_limit_bytes=16 * 1024 * 1024),
        cost_estimate=pl.CostEstimate(flops=flops, bytes_accessed=traffic, transcendentals=0),
        name=name,
    )(*operands, *after)


def body(features, tiles, weight, cotangent, send_count, send_index, cross_dst, cross_weight):
    rows, width = features.shape
    groups = lax.axis_size("comm")
    blocks = lax.axis_size("blk")
    slots = send_index.shape[1]
    per_peer = slots // groups
    nodes = rows * groups * blocks
    array = jax.ShapeDtypeStruct
    work = 2 * rows * slots * width

    def shift(value, step):
        pairs = [(i, (i + step) % blocks) for i in range(blocks)]
        return lax.ppermute(value, "blk", pairs)

    def exchange(value):
        return lax.all_to_all(value, "comm", split_axis=0, concat_axis=0, tiled=True)

    both = ("comm", "blk")
    devices = groups * blocks
    outer = min(4, groups // 2)
    chunks = devices // outer
    share = width // chunks
    low, high = blocks.bit_length() - 1, chunks.bit_length() - 1
    others = list(range(low)) + list(range(low + 1, high))
    pairs = [others[i : i + 2] for i in range(0, len(others), 2)]

    core = 1 << low
    outer_bits = list(range(high, devices.bit_length() - 1))

    def masks(bits, straight=()):
        plain = [sum((i >> j & 1) << bit for j, bit in enumerate(bits)) for i in range(1 << len(bits))]
        if bits is outer_bits:
            return [mask ^ core * (i.bit_count() % 2) for i, mask in enumerate(plain)]
        return [mask if mask in (0, core) or mask in straight else mask ^ core for mask in plain]

    def order_of(straight=()):
        order = [0]
        for bits in reversed([[low]] + pairs):
            order = [mask ^ place for mask in masks(bits, straight) for place in order]
        return order

    straight = (1,) if blocks == 2 else ()
    order, gather_order = order_of(straight), order_of()
    way_bits = [sum(1 << bit - low - 1 for bit in bits if bit > low) for bits in pairs]
    parities = [
        (sum(bool(chip & bits) for bits in way_bits) + (chip >> high - low - 1).bit_count()) % 2
        for chip in range(groups // 2)
    ]

    def swap(value, mask):
        return lax.ppermute(value, both, [(i, i ^ mask) for i in range(devices)]) if mask else value

    far = jnp.stack([shift(features, -step) for step in range(1, blocks)])
    own, give, chosen = kernel(
        gather_kernel,
        "gather",
        (
            array((groups // 2, per_peer, width), F32),
            array((groups // 2, per_peer, width), F32),
            array((rows, slots), BF16),
        ),
        (send_count, send_index, features),
        spec=HBM,
        scratch=(
            pltpu.VMEM(send_count.shape, jnp.int32),
            pltpu.VMEM(send_index.shape, jnp.int32),
            pltpu.VMEM(features.shape, F32),
            pltpu.VMEM((slots, width), F32),
            pltpu.SemaphoreType.DMA((3,)),
        ),
        flops=work,
        traffic=4 * (rows + slots) * width,
    )
    got = swap(give, 1 << low)
    packed = jnp.stack([own, got], axis=1)
    arrived = [swap(packed[mask], 2 * mask + 1 << low) for mask in range(1, groups // 2)]
    local, cross, tile_parts, weight_parts = kernel(
        prepare_kernel,
        "prepare",
        (
            array((rows, width), F32),
            array((2, rows, slots), BF16),
            array((blocks, 2, rows, rows), BF16),
            array((2, width, width), BF16),
        ),
        (features, far, tiles, weight, cross_dst, cross_weight),
        flops=3 * work,
        traffic=4 * (4 * rows + width) * width,
    )
    aligned = share % 8 == 0
    half = width // 2
    held = array((slots // 2 + (half if aligned else 0), width), F32)
    value, spread, keep, give, *partial = kernel(
        functools.partial(layer_kernel, order, parities),
        "layer",
        (array((rows, width), F32), array((2, rows, width), BF16), held, held)
        + (() if aligned else (array((width, width), F32),)),
        (local, cross, weight_parts, cotangent, own, got, *arrived),
        scratch=(pltpu.VMEM((slots, width), F32), pltpu.VMEM((width, width), F32)),
        flops=15 * work,
        traffic=4 * (4 * rows + 2 * slots) * width,
    )
    if not aligned:
        ordered = partial[0].reshape(chunks, share, width)[chunk_number(chunks) ^ jnp.array(order)]
        keep = jnp.concatenate([ordered[: chunks // 2].reshape(half, width), keep])
        give = jnp.concatenate([ordered[chunks // 2 :].reshape(half, width), give])
    inner, leaving, output = kernel(
        inner_kernel,
        "inner",
        (array((rows, width), F32), array((blocks - 1, rows, width), F32), array((rows, width), F32)),
        (tile_parts, spread, value),
        flops=3 * work,
        traffic=4 * 6 * rows * width,
    )

    arrays = [keep, give, swap(give, 1 << low)]
    terms = [[(0, i * share, share), (2, i * share, share)] for i in range(chunks // 2)]
    moving = {
        2 * m + parities[m]: [(k, (2 * k, half + m * per_peer, per_peer)) for k in range(2)]
        for m in range(groups // 2)
    }
    far_pieces = []

    def pack(name, layout, scale=None, after=()):
        used = sorted({leaf[0] for pieces in layout for leaf in leaves(pieces)})
        layout = [[renumber(piece, used) for piece in pieces] for pieces in layout]
        out = tuple(array((sum(map(rows_of, pieces)), width), F32) for pieces in layout)
        operands = [arrays[i] for i in used]
        traffic = 8 * width * sum(o.shape[0] for o in out)
        return kernel(functools.partial(pack_kernel, layout, scale, len(used)), name, out, operands, traffic=traffic, after=after)

    all_outer = sum(1 << bit for bit in outer_bits) >> low
    early = ()
    for bits in pairs + [outer_bits]:
        last = bits is outer_bits
        keeps = len(terms) if last else len(terms) >> len(bits)
        layout, riders = [], []
        partners = list(enumerate(masks(bits, straight)))[:0:-1]
        for i, mask in partners:
            pieces = list(terms) if last else terms[i * keeps : (i + 1) * keeps]
            way, across = mask >> low, mask & (core - 1)
            all_ways = sum(1 << bit for bit in bits) >> low
            going = [q for q in sorted(moving) if not across and q & all_ways == way & all_ways]
            riders.append([(q, come) for q in going for come, _ in moving[q]])
            pieces += [piece for q in going for _, piece in moving[q]]
            if blocks == 2 and mask == 1:
                arrays.append(leaving[0])
                pieces.append((len(arrays) - 1, 0, rows))
            layout.append(pieces)
        leaders = masks(outer_bits)[:1:-1] if bits is pairs[-1] else []
        for mask in leaders:
            way = mask >> low
            going = [q for q in sorted(moving) if q & ~1 == way & all_outer]
            riders.append([(q, come) for q in going for come, _ in moving[q]])
            layout.append([piece for q in going for _, piece in moving[q]])
        sent = pack("pack", layout, after=early)
        came, count = [], len(partners)
        partners = [mask for _, mask in partners] + leaders
        for q in {q for rides in riders for q, _ in rides}:
            del moving[q]
        for i, (mask, value, rides) in enumerate(zip(partners, sent, riders)):
            arrays.append(swap(value, mask))
            number, first = len(arrays) - 1, 0
            if i < count:
                came.append([(number, j * share, share) for j in range(keeps)])
                first = keeps * share
            for q, come in rides:
                way = mask >> low
                moving.setdefault(q ^ way, []).append((come ^ way, (number, first, per_peer)))
                first += per_peer
            if blocks == 2 and mask == 1:
                far_pieces.append((number, first, rows))
        early = tuple(arrays[len(arrays) - len(leaders) :]) if leaders else ()
        terms = [[terms[j]] + [pieces[j] for pieces in reversed(came)] for j in range(keeps)]
    if blocks > 2:
        for step in range(1, blocks):
            arrays.append(shift(leaving[step - 1], step))
            far_pieces.append((len(arrays) - 1, 0, rows))

    sums = pack("sum", [terms], nodes ** (-0.5))[0].reshape(1, share, width)
    for bits in reversed(pairs):
        sums = jnp.concatenate([swap(sums, mask) for mask in masks(bits)])
    other = swap(sums, 1 << low)
    if aligned:
        grad_weight = kernel(
            functools.partial(place_kernel, gather_order),
            "place",
            array((width, width), F32),
            (sums, other),
            traffic=8 * width * width,
        )
    else:
        places = jnp.array([gather_order.index(i) for i in range(chunks)])[chunk_number(chunks) ^ jnp.arange(chunks)]
        grad_weight = jnp.concatenate([sums, other])[places].reshape(width, width)

    came = moving[0]
    used = sorted({piece[0] for _, piece in came} | {piece[0] for piece in far_pieces})
    grad_features = kernel(
        functools.partial(
            finish_kernel,
            [(distance, renumber(piece, used)) for distance, piece in came],
            [renumber(piece, used) for piece in far_pieces],
        ),
        "finish",
        array((rows, width), F32),
        (chosen, inner, *(arrays[i] for i in used)),
        scratch=(pltpu.VMEM((slots, width), F32),),
        flops=2 * work,
        traffic=4 * (3 * rows + slots) * width,
    )
    return (output, grad_features, grad_weight)


def solution(mesh):
    return jax.shard_map(
        body,
        mesh=mesh,
        in_specs=(
            P(("comm", "blk"), None),
            P(("comm", "blk"), None),
            P(),
            P(("comm", "blk"), None),
            P(("comm", "blk"), None),
            P(("comm", "blk"), None),
            P(("comm", "blk"), None),
            P(("comm", "blk"), None),
        ),
        out_specs=(P(("comm", "blk"), None), P(("comm", "blk"), None), P()),
        check_vma=False,
    )
```

```python
import functools
import math

import jax
import jax.numpy as jnp
from jax import lax
from jax.experimental import pallas as pl
from jax.experimental.pallas import tpu as pltpu
from jax.sharding import PartitionSpec as P

F32 = jnp.float32
BF16 = jnp.bfloat16
VMEM = pl.BlockSpec(memory_space=pltpu.VMEM)
HBM = pl.BlockSpec(memory_space=pltpu.HBM)


def split(value):
    high = value.astype(BF16)
    return high, (value - high.astype(F32)).astype(BF16)


def product(a, b, dims):
    return lax.dot_general(a, b, (dims, ((), ())), preferred_element_type=F32)


def dot3(a, b, dims=((1,), (0,))):
    (a_high, a_low), (b_high, b_low) = a, b
    return (product(a_low, b_high, dims) + product(a_high, b_low, dims)) + product(a_high, b_high, dims)


def dot_onehot(a, b, dims):
    return product(a, b[1], dims) + product(a, b[0], dims)


def tree(terms):
    while len(terms) > 1:
        terms = [terms[i] + terms[i + 1] for i in range(0, len(terms), 2)]
    return terms[0]


def send_matrix(counts, index, rows):
    groups, slots = counts.shape[1], index.shape[1]
    per_peer = slots // groups
    lane = lax.broadcasted_iota(jnp.int32, (groups, slots), 1)
    first = lax.broadcasted_iota(jnp.int32, (groups, slots), 0) * per_peer
    of_peer = ((lane >= first) & (lane < first + per_peer)).astype(F32)
    limit = jnp.dot(counts.astype(F32), of_peer, preferred_element_type=F32)
    place = lax.broadcasted_iota(jnp.int32, (1, slots), 1) % per_peer
    chosen = jnp.where(place.astype(F32) < limit, index, -1)
    return (lax.broadcasted_iota(jnp.int32, (rows, slots), 0) == chosen).astype(F32).astype(BF16)


def gather_kernel(
    count_hbm, index_hbm, features_hbm, own_ref, give_ref, chosen_ref, count_ref, index_ref, features_ref, rows_ref, sems
):
    pairs = ((count_hbm, count_ref), (index_hbm, index_ref), (features_hbm, features_ref))
    copies = [pltpu.make_async_copy(source, target, sems.at[i]) for i, (source, target) in enumerate(pairs)]
    for copy in copies:
        copy.start()
    copies[0].wait()
    copies[1].wait()
    chosen = send_matrix(count_ref[...], index_ref[...], features_ref.shape[0])
    chosen_ref[...] = chosen
    copies[2].wait()
    rows_ref[...] = dot_onehot(chosen, split(features_ref[...]), ((0,), (0,)))
    me = lax.axis_index("comm")
    chips, per_peer = own_ref.shape[:2]
    for mask in range(chips):
        for k, out_ref in enumerate((own_ref, give_ref)):
            start = lax.bitwise_xor(me, 2 * mask + (k ^ (mask > 0))) * per_peer
            out_ref[mask] = rows_ref[pl.ds(pl.multiple_of(start, per_peer), per_peer), :]


def prepare_kernel(
    near_ref, far_ref, tiles_ref, weight_ref, target_ref, edge_ref,
    local_ref, cross_ref, tiles_out, weight_out,
):
    rows = near_ref.shape[0]
    blocks = far_ref.shape[0] + 1
    slots = target_ref.shape[1]
    me = lax.axis_index("blk")

    total = None
    for step in range(blocks):
        start = lax.rem(me + step, blocks) * rows
        tile = split(tiles_ref[:, pl.ds(pl.multiple_of(start, rows), rows)])
        tiles_out[step, 0], tiles_out[step, 1] = tile
        term = dot3(tile, split(near_ref[...] if step == 0 else far_ref[step - 1]))
        total = term if total is None else total + term
    local_ref[...] = total
    hit = lax.broadcasted_iota(jnp.int32, (rows, slots), 0) == target_ref[...]
    cross_ref[0], cross_ref[1] = split(jnp.where(hit, edge_ref[...], 0.0))
    weight_out[0], weight_out[1] = split(weight_ref[...])


def chunk_number(chunks):
    blocks = lax.axis_size("blk")
    number = lax.axis_index("comm") * blocks + lax.axis_index("blk")
    outer = lax.div(number, chunks)
    crossed = lax.rem(outer + lax.div(outer, 2), 2) * blocks
    return lax.bitwise_xor(lax.rem(number, chunks), crossed)


def layer_kernel(
    order, parities, arrival, local_ref, cross_ref, weight_ref, cotangent_ref, own_ref, got_ref, *refs
):
    chips, per_peer = own_ref.shape[:2]
    arrived_refs, refs = refs[: chips - 1], refs[chips - 1 :]
    out_ref, spread_ref, keep_ref, give_ref, *partial_refs, slots_ref, terms_ref = refs
    peer = lax.axis_index("comm")
    for mask in range(chips):
        for k in range(2):
            start = lax.bitwise_xor(peer, 2 * mask + (k ^ (mask > 0))) * per_peer
            block = arrived_refs[arrival.index(mask - 1)][k] if mask else (got_ref if k else own_ref)[0]
            slots_ref[pl.ds(pl.multiple_of(start, per_peer), per_peer), :] = block
    cross = cross_ref[0], cross_ref[1]
    weight = weight_ref[0], weight_ref[1]

    aggregated = split(local_ref[...] + dot3(cross, split(slots_ref[...])))
    pre = dot3(aggregated, weight)
    cdf = 0.5 * (1.0 + lax.erf(pre * math.sqrt(0.5)))
    density = jnp.exp(-0.5 * pre * pre) * (1.0 / math.sqrt(2.0 * math.pi))
    grad_pre = split(cotangent_ref[...] * (cdf + pre * density))
    out_ref[...] = pre * cdf
    terms_ref[...] = dot3(aggregated, grad_pre, ((0,), (0,)))
    spread = split(dot3(grad_pre, weight, ((1,), (1,))))
    spread_ref[0], spread_ref[1] = spread
    slots_ref[...] = dot3(cross, spread, ((0,), (0,)))

    half = 0
    if partial_refs:
        partial_refs[0][...] = terms_ref[...]
    else:
        half = terms_ref.shape[0] // 2
        share = terms_ref.shape[0] // len(order)
        me = chunk_number(len(order))
        for place, relative in enumerate(order):
            start = lax.bitwise_xor(me, relative) * share
            chunk = terms_ref[pl.ds(pl.multiple_of(start, share), share), :]
            target_ref = keep_ref if place < len(order) // 2 else give_ref
            target_ref[pl.ds(place * share % half, share), :] = chunk
    for mask in range(chips):
        for k, target_ref in enumerate((keep_ref, give_ref)):
            start = lax.bitwise_xor(peer, 2 * mask + (k ^ parities[mask])) * per_peer
            block = slots_ref[pl.ds(pl.multiple_of(start, per_peer), per_peer), :]
            target_ref[pl.ds(half + mask * per_peer, per_peer), :] = block


def place_kernel(order, mine_ref, other_ref, out_ref):
    half, share = mine_ref.shape[:2]
    me = chunk_number(len(order))
    for i, relative in enumerate(order):
        start = lax.bitwise_xor(me, relative) * share
        out_ref[pl.ds(pl.multiple_of(start, share), share), :] = mine_ref[i] if i < half else other_ref[i - half]


def inner_kernel(tiles_ref, spread_ref, value_ref, near_ref, far_ref, out_ref):
    spread = spread_ref[0], spread_ref[1]
    for step in range(far_ref.shape[0]):
        far_ref[step] = dot3((tiles_ref[step + 1, 0], tiles_ref[step + 1, 1]), spread, ((0,), (0,)))
    near_ref[...] = dot3((tiles_ref[0, 0], tiles_ref[0, 1]), spread, ((0,), (0,)))
    out_ref[...] = value_ref[...]


def value_of(piece, refs):
    if isinstance(piece, list):
        return tree([value_of(term, refs) for term in piece])
    source, first, rows = piece
    return refs[source][first : first + rows, :]


def rows_of(piece):
    return rows_of(piece[0]) if isinstance(piece, list) else piece[2]


def leaves(piece):
    return [leaf for term in piece for leaf in leaves(term)] if isinstance(piece, list) else [piece]


def renumber(piece, used):
    if isinstance(piece, list):
        return [renumber(term, used) for term in piece]
    return (used.index(piece[0]), *piece[1:])


def pack_kernel(layout, scale, count, *refs):
    for pieces, out_ref in zip(layout, refs[count:]):
        first = 0
        for piece in pieces:
            rows = rows_of(piece)
            value = value_of(piece, refs)
            out_ref[first : first + rows, :] = value if scale is None else value * scale
            first += rows


def finish_kernel(blocks, far, chosen_ref, near_ref, *refs):
    *refs, grad_ref, slots_ref = refs
    peer = lax.axis_index("comm")
    for distance, piece in blocks:
        rows = piece[2]
        start = lax.bitwise_xor(peer, distance) * rows
        slots_ref[pl.ds(pl.multiple_of(start, rows), rows), :] = value_of(piece, refs)
    total = near_ref[...]
    for piece in far:
        total += value_of(piece, refs)
    grad_ref[...] = total + dot_onehot(chosen_ref[...], split(slots_ref[...]), ((1,), (0,)))


def kernel(body, name, out, operands, spec=VMEM, scratch=(), flops=0, traffic=0, after=()):
    count = len(operands)
    if spec is HBM:
        operands = [pltpu.with_memory_space_constraint(x, pltpu.HBM) for x in operands]
    return pl.pallas_call(
        lambda *refs: body(*refs[:count], *refs[count + len(after) :]),
        out_shape=out,
        in_specs=[spec] * count + [pl.BlockSpec(memory_space=pl.ANY)] * len(after),
        out_specs=jax.tree.map(lambda _: VMEM, out),
        scratch_shapes=list(scratch),
        compiler_params=pltpu.CompilerParams(vmem_limit_bytes=16 * 1024 * 1024),
        cost_estimate=pl.CostEstimate(flops=flops, bytes_accessed=traffic, transcendentals=0),
        name=name,
    )(*operands, *after)


def body(features, tiles, weight, cotangent, send_count, send_index, cross_dst, cross_weight):
    rows, width = features.shape
    groups = lax.axis_size("comm")
    blocks = lax.axis_size("blk")
    slots = send_index.shape[1]
    per_peer = slots // groups
    nodes = rows * groups * blocks
    array = jax.ShapeDtypeStruct
    work = 2 * rows * slots * width

    def shift(value, step):
        pairs = [(i, (i + step) % blocks) for i in range(blocks)]
        return lax.ppermute(value, "blk", pairs)

    def exchange(value):
        return lax.all_to_all(value, "comm", split_axis=0, concat_axis=0, tiled=True)

    both = ("comm", "blk")
    devices = groups * blocks
    outer = min(4, groups // 2)
    chunks = devices // outer
    share = width // chunks
    low, high = blocks.bit_length() - 1, chunks.bit_length() - 1
    others = list(range(low)) + list(range(low + 1, high))
    pairs = [others[i : i + 2] for i in range(0, len(others), 2)]

    core = 1 << low
    outer_bits = list(range(high, devices.bit_length() - 1))

    def masks(bits, straight=()):
        plain = [sum((i >> j & 1) << bit for j, bit in enumerate(bits)) for i in range(1 << len(bits))]
        if bits is outer_bits:
            return [mask ^ core * (i.bit_count() % 2) for i, mask in enumerate(plain)]
        return [mask if mask in (0, core) or mask in straight else mask ^ core for mask in plain]

    def order_of(straight=()):
        order = [0]
        for bits in reversed([[low]] + pairs):
            order = [mask ^ place for mask in masks(bits, straight) for place in order]
        return order

    straight = (1,) if blocks == 2 else ()
    order, gather_order = order_of(straight), order_of()
    way_bits = [sum(1 << bit - low - 1 for bit in bits if bit > low) for bits in pairs]
    parities = [
        (sum(bool(chip & bits) for bits in way_bits) + (chip >> high - low - 1).bit_count()) % 2
        for chip in range(groups // 2)
    ]

    def swap(value, mask):
        return lax.ppermute(value, both, [(i, i ^ mask) for i in range(devices)]) if mask else value

    far = jnp.stack([shift(features, -step) for step in range(1, blocks)])
    own, give, chosen = kernel(
        gather_kernel,
        "gather",
        (
            array((groups // 2, per_peer, width), F32),
            array((groups // 2, per_peer, width), F32),
            array((rows, slots), BF16),
        ),
        (send_count, send_index, features),
        spec=HBM,
        scratch=(
            pltpu.VMEM(send_count.shape, jnp.int32),
            pltpu.VMEM(send_index.shape, jnp.int32),
            pltpu.VMEM(features.shape, F32),
            pltpu.VMEM((slots, width), F32),
            pltpu.SemaphoreType.DMA((3,)),
        ),
        flops=work,
        traffic=4 * (rows + slots) * width,
    )
    got = swap(give, 1 << low)
    packed = jnp.stack([own, got], axis=1)
    arrived = [swap(packed[mask], 2 * mask + 1 << low) for mask in range(1, groups // 2)]
    arrival = list(range(groups // 2 - 1))
    arrival.append(arrival.pop(groups // 4 - 1))
    local, cross, tile_parts, weight_parts = kernel(
        prepare_kernel,
        "prepare",
        (
            array((rows, width), F32),
            array((2, rows, slots), BF16),
            array((blocks, 2, rows, rows), BF16),
            array((2, width, width), BF16),
        ),
        (features, far, tiles, weight, cross_dst, cross_weight),
        flops=3 * work,
        traffic=4 * (4 * rows + width) * width,
    )
    aligned = share % 8 == 0
    half = width // 2
    held = array((slots // 2 + (half if aligned else 0), width), F32)
    value, spread, keep, give, *partial = kernel(
        functools.partial(layer_kernel, order, parities, arrival),
        "layer",
        (array((rows, width), F32), array((2, rows, width), BF16), held, held)
        + (() if aligned else (array((width, width), F32),)),
        (local, cross, weight_parts, cotangent, own, got, *(arrived[i] for i in arrival)),
        scratch=(pltpu.VMEM((slots, width), F32), pltpu.VMEM((width, width), F32)),
        flops=15 * work,
        traffic=4 * (4 * rows + 2 * slots) * width,
    )
    if not aligned:
        ordered = partial[0].reshape(chunks, share, width)[chunk_number(chunks) ^ jnp.array(order)]
        keep = jnp.concatenate([ordered[: chunks // 2].reshape(half, width), keep])
        give = jnp.concatenate([ordered[chunks // 2 :].reshape(half, width), give])
    inner, leaving, output = kernel(
        inner_kernel,
        "inner",
        (array((rows, width), F32), array((blocks - 1, rows, width), F32), array((rows, width), F32)),
        (tile_parts, spread, value),
        flops=3 * work,
        traffic=4 * 6 * rows * width,
    )

    arrays = [keep, give, swap(give, 1 << low)]
    terms = [[(0, i * share, share), (2, i * share, share)] for i in range(chunks // 2)]
    moving = {
        2 * m + parities[m]: [(k, (2 * k, half + m * per_peer, per_peer)) for k in range(2)]
        for m in range(groups // 2)
    }
    far_pieces = []

    def pack(name, layout, scale=None):
        used = sorted({leaf[0] for pieces in layout for leaf in leaves(pieces)})
        layout = [[renumber(piece, used) for piece in pieces] for pieces in layout]
        out = tuple(array((sum(map(rows_of, pieces)), width), F32) for pieces in layout)
        operands = [arrays[i] for i in used]
        traffic = 8 * width * sum(o.shape[0] for o in out)
        return kernel(functools.partial(pack_kernel, layout, scale, len(used)), name, out, operands, traffic=traffic)

    for bits in pairs + [outer_bits]:
        last = bits is outer_bits
        keeps = len(terms) if last else len(terms) >> len(bits)
        layout, riders = [], []
        partners = list(enumerate(masks(bits, straight)))[:0:-1]
        if last:
            partners.sort(key=lambda partner: partner[0] != 2)
        for i, mask in partners:
            pieces = list(terms) if last else terms[i * keeps : (i + 1) * keeps]
            way, across = mask >> low, mask & (core - 1)
            all_ways = sum(1 << bit for bit in bits) >> low
            going = [q for q in sorted(moving) if not across and q & all_ways == way & all_ways]
            riders.append([(q, come) for q in going for come, _ in moving[q]])
            pieces += [piece for q in going for _, piece in moving[q]]
            if blocks == 2 and mask == 1:
                arrays.append(leaving[0])
                pieces.append((len(arrays) - 1, 0, rows))
            layout.append(pieces)
        sent = pack("pack", layout)
        came = {}
        for (i, mask), value, rides in zip(partners, sent, riders):
            arrays.append(swap(value, mask))
            number, first = len(arrays) - 1, 0
            came[i] = [(number, j * share, share) for j in range(keeps)]
            first = keeps * share
            for q, come in rides:
                way = mask >> low
                moving.setdefault(q ^ way, []).append((come ^ way, (number, first, per_peer)))
                first += per_peer
            if blocks == 2 and mask == 1:
                far_pieces.append((number, first, rows))
            for q in {q for q, _ in rides}:
                del moving[q]
        terms = [[terms[j]] + [came[i][j] for i in sorted(came)] for j in range(keeps)]
    if blocks > 2:
        for step in range(1, blocks):
            arrays.append(shift(leaving[step - 1], step))
            far_pieces.append((len(arrays) - 1, 0, rows))

    sums = pack("sum", [terms], nodes ** (-0.5))[0].reshape(1, share, width)
    for bits in reversed(pairs):
        sums = jnp.concatenate([swap(sums, mask) for mask in masks(bits)])
    other = swap(sums, 1 << low)
    if aligned:
        grad_weight = kernel(
            functools.partial(place_kernel, gather_order),
            "place",
            array((width, width), F32),
            (sums, other),
            traffic=8 * width * width,
        )
    else:
        places = jnp.array([gather_order.index(i) for i in range(chunks)])[chunk_number(chunks) ^ jnp.arange(chunks)]
        grad_weight = jnp.concatenate([sums, other])[places].reshape(width, width)

    came = moving[0]
    used = sorted({piece[0] for _, piece in came} | {piece[0] for piece in far_pieces})
    grad_features = kernel(
        functools.partial(
            finish_kernel,
            [(distance, renumber(piece, used)) for distance, piece in came],
            [renumber(piece, used) for piece in far_pieces],
        ),
        "finish",
        array((rows, width), F32),
        (chosen, inner, *(arrays[i] for i in used)),
        scratch=(pltpu.VMEM((slots, width), F32),),
        flops=2 * work,
        traffic=4 * (3 * rows + slots) * width,
    )
    return (output, grad_features, grad_weight)


def solution(mesh):
    return jax.shard_map(
        body,
        mesh=mesh,
        in_specs=(
            P(("comm", "blk"), None),
            P(("comm", "blk"), None),
            P(),
            P(("comm", "blk"), None),
            P(("comm", "blk"), None),
            P(("comm", "blk"), None),
            P(("comm", "blk"), None),
            P(("comm", "blk"), None),
        ),
        out_specs=(P(("comm", "blk"), None), P(("comm", "blk"), None), P()),
        check_vma=False,
    )
```

```python
import functools
import math

import jax
import jax.numpy as jnp
from jax import lax
from jax.experimental import pallas as pl
from jax.experimental.pallas import tpu as pltpu
from jax.sharding import PartitionSpec as P

F32 = jnp.float32
BF16 = jnp.bfloat16
VMEM = pl.BlockSpec(memory_space=pltpu.VMEM)
HBM = pl.BlockSpec(memory_space=pltpu.HBM)


def split(value):
    high = value.astype(BF16)
    return high, (value - high.astype(F32)).astype(BF16)


def product(a, b, dims):
    return lax.dot_general(a, b, (dims, ((), ())), preferred_element_type=F32)


def dot3(a, b, dims=((1,), (0,))):
    (a_high, a_low), (b_high, b_low) = a, b
    return (product(a_low, b_high, dims) + product(a_high, b_low, dims)) + product(a_high, b_high, dims)


def dot_onehot(a, b, dims):
    return product(a, b[1], dims) + product(a, b[0], dims)


def tree(terms):
    while len(terms) > 1:
        terms = [terms[i] + terms[i + 1] for i in range(0, len(terms), 2)]
    return terms[0]


def send_matrix(counts, index, rows):
    groups, slots = counts.shape[1], index.shape[1]
    per_peer = slots // groups
    lane = lax.broadcasted_iota(jnp.int32, (groups, slots), 1)
    first = lax.broadcasted_iota(jnp.int32, (groups, slots), 0) * per_peer
    of_peer = ((lane >= first) & (lane < first + per_peer)).astype(F32)
    limit = jnp.dot(counts.astype(F32), of_peer, preferred_element_type=F32)
    place = lax.broadcasted_iota(jnp.int32, (1, slots), 1) % per_peer
    chosen = jnp.where(place.astype(F32) < limit, index, -1)
    return (lax.broadcasted_iota(jnp.int32, (rows, slots), 0) == chosen).astype(F32).astype(BF16)


def gather_kernel(
    count_hbm, index_hbm, features_hbm, own_ref, give_ref, chosen_ref, count_ref, index_ref, features_ref, rows_ref, sems
):
    pairs = ((count_hbm, count_ref), (index_hbm, index_ref), (features_hbm, features_ref))
    copies = [pltpu.make_async_copy(source, target, sems.at[i]) for i, (source, target) in enumerate(pairs)]
    for copy in copies:
        copy.start()
    copies[0].wait()
    copies[1].wait()
    chosen = send_matrix(count_ref[...], index_ref[...], features_ref.shape[0])
    chosen_ref[...] = chosen
    copies[2].wait()
    rows_ref[...] = dot_onehot(chosen, split(features_ref[...]), ((0,), (0,)))
    me = lax.axis_index("comm")
    chips, per_peer = own_ref.shape[:2]
    for mask in range(chips):
        for k, out_ref in enumerate((own_ref, give_ref)):
            start = lax.bitwise_xor(me, 2 * mask + (k ^ (mask > 0))) * per_peer
            out_ref[mask] = rows_ref[pl.ds(pl.multiple_of(start, per_peer), per_peer), :]


def prepare_kernel(
    near_ref, far_ref, tiles_ref, weight_ref, target_ref, edge_ref,
    local_ref, cross_ref, tiles_out, weight_out,
):
    rows = near_ref.shape[0]
    blocks = far_ref.shape[0] + 1
    slots = target_ref.shape[1]
    me = lax.axis_index("blk")

    total = None
    for step in range(blocks):
        start = lax.rem(me + step, blocks) * rows
        tile = split(tiles_ref[:, pl.ds(pl.multiple_of(start, rows), rows)])
        tiles_out[step, 0], tiles_out[step, 1] = tile
        term = dot3(tile, split(near_ref[...] if step == 0 else far_ref[step - 1]))
        total = term if total is None else total + term
    local_ref[...] = total
    hit = lax.broadcasted_iota(jnp.int32, (rows, slots), 0) == target_ref[...]
    cross_ref[0], cross_ref[1] = split(jnp.where(hit, edge_ref[...], 0.0))
    weight_out[0], weight_out[1] = split(weight_ref[...])


def chunk_number(chunks):
    blocks = lax.axis_size("blk")
    number = lax.axis_index("comm") * blocks + lax.axis_index("blk")
    outer = lax.div(number, chunks)
    crossed = lax.rem(outer + lax.div(outer, 2), 2) * blocks
    return lax.bitwise_xor(lax.rem(number, chunks), crossed)


def layer_kernel(
    order, parities, arrival, local_ref, cross_ref, weight_ref, cotangent_ref, own_ref, got_ref, *refs
):
    chips, per_peer = own_ref.shape[:2]
    arrived_refs, refs = refs[: chips - 1], refs[chips - 1 :]
    out_ref, spread_ref, keep_ref, give_ref, *partial_refs, slots_ref, terms_ref = refs
    peer = lax.axis_index("comm")
    for mask in range(chips):
        for k in range(2):
            start = lax.bitwise_xor(peer, 2 * mask + (k ^ (mask > 0))) * per_peer
            block = arrived_refs[arrival.index(mask - 1)][k] if mask else (got_ref if k else own_ref)[0]
            slots_ref[pl.ds(pl.multiple_of(start, per_peer), per_peer), :] = block
    cross = cross_ref[0], cross_ref[1]
    weight = weight_ref[0], weight_ref[1]

    aggregated = split(local_ref[...] + dot3(cross, split(slots_ref[...])))
    pre = dot3(aggregated, weight)
    cdf = 0.5 * (1.0 + lax.erf(pre * math.sqrt(0.5)))
    density = jnp.exp(-0.5 * pre * pre) * (1.0 / math.sqrt(2.0 * math.pi))
    grad_pre = split(cotangent_ref[...] * (cdf + pre * density))
    out_ref[...] = pre * cdf
    terms_ref[...] = dot3(aggregated, grad_pre, ((0,), (0,)))
    spread = split(dot3(grad_pre, weight, ((1,), (1,))))
    spread_ref[0], spread_ref[1] = spread
    slots_ref[...] = dot3(cross, spread, ((0,), (0,)))

    half = 0
    if partial_refs:
        partial_refs[0][...] = terms_ref[...]
    else:
        half = terms_ref.shape[0] // 2
        share = terms_ref.shape[0] // len(order)
        me = chunk_number(len(order))
        for place, relative in enumerate(order):
            start = lax.bitwise_xor(me, relative) * share
            chunk = terms_ref[pl.ds(pl.multiple_of(start, share), share), :]
            target_ref = keep_ref if place < len(order) // 2 else give_ref
            target_ref[pl.ds(place * share % half, share), :] = chunk
    for mask in range(chips):
        for k, target_ref in enumerate((keep_ref, give_ref)):
            start = lax.bitwise_xor(peer, 2 * mask + (k ^ parities[mask])) * per_peer
            block = slots_ref[pl.ds(pl.multiple_of(start, per_peer), per_peer), :]
            target_ref[pl.ds(half + mask * per_peer, per_peer), :] = block


def place_kernel(order, mine_ref, other_ref, out_ref):
    half, share = mine_ref.shape[:2]
    me = chunk_number(len(order))
    for i, relative in enumerate(order):
        start = lax.bitwise_xor(me, relative) * share
        out_ref[pl.ds(pl.multiple_of(start, share), share), :] = mine_ref[i] if i < half else other_ref[i - half]


def inner_kernel(tiles_ref, spread_ref, value_ref, near_ref, far_ref, out_ref):
    spread = spread_ref[0], spread_ref[1]
    for step in range(far_ref.shape[0]):
        far_ref[step] = dot3((tiles_ref[step + 1, 0], tiles_ref[step + 1, 1]), spread, ((0,), (0,)))
    near_ref[...] = dot3((tiles_ref[0, 0], tiles_ref[0, 1]), spread, ((0,), (0,)))
    out_ref[...] = value_ref[...]


def value_of(piece, refs):
    if isinstance(piece, list):
        return tree([value_of(term, refs) for term in piece])
    source, first, rows = piece
    return refs[source][first : first + rows, :]


def rows_of(piece):
    return rows_of(piece[0]) if isinstance(piece, list) else piece[2]


def leaves(piece):
    return [leaf for term in piece for leaf in leaves(term)] if isinstance(piece, list) else [piece]


def renumber(piece, used):
    if isinstance(piece, list):
        return [renumber(term, used) for term in piece]
    return (used.index(piece[0]), *piece[1:])


def pack_kernel(layout, scale, count, *refs):
    for pieces, out_ref in zip(layout, refs[count:]):
        first = 0
        for piece in pieces:
            rows = rows_of(piece)
            value = value_of(piece, refs)
            out_ref[first : first + rows, :] = value if scale is None else value * scale
            first += rows


def finish_kernel(blocks, far, chosen_ref, near_ref, *refs):
    *refs, grad_ref, slots_ref = refs
    peer = lax.axis_index("comm")
    for distance, piece in blocks:
        rows = piece[2]
        start = lax.bitwise_xor(peer, distance) * rows
        slots_ref[pl.ds(pl.multiple_of(start, rows), rows), :] = value_of(piece, refs)
    total = near_ref[...]
    for piece in far:
        total += value_of(piece, refs)
    grad_ref[...] = total + dot_onehot(chosen_ref[...], split(slots_ref[...]), ((1,), (0,)))


def kernel(body, name, out, operands, spec=VMEM, scratch=(), flops=0, traffic=0, after=()):
    count = len(operands)
    if spec is HBM:
        operands = [pltpu.with_memory_space_constraint(x, pltpu.HBM) for x in operands]
    return pl.pallas_call(
        lambda *refs: body(*refs[:count], *refs[count + len(after) :]),
        out_shape=out,
        in_specs=[spec] * count + [pl.BlockSpec(memory_space=pl.ANY)] * len(after),
        out_specs=jax.tree.map(lambda _: VMEM, out),
        scratch_shapes=list(scratch),
        compiler_params=pltpu.CompilerParams(vmem_limit_bytes=16 * 1024 * 1024),
        cost_estimate=pl.CostEstimate(flops=flops, bytes_accessed=traffic, transcendentals=0),
        name=name,
    )(*operands, *after)


def body(features, tiles, weight, cotangent, send_count, send_index, cross_dst, cross_weight):
    rows, width = features.shape
    groups = lax.axis_size("comm")
    blocks = lax.axis_size("blk")
    slots = send_index.shape[1]
    per_peer = slots // groups
    nodes = rows * groups * blocks
    array = jax.ShapeDtypeStruct
    work = 2 * rows * slots * width

    def shift(value, step):
        pairs = [(i, (i + step) % blocks) for i in range(blocks)]
        return lax.ppermute(value, "blk", pairs)

    def exchange(value):
        return lax.all_to_all(value, "comm", split_axis=0, concat_axis=0, tiled=True)

    both = ("comm", "blk")
    devices = groups * blocks
    outer = min(4, groups // 2)
    chunks = devices // outer
    share = width // chunks
    low, high = blocks.bit_length() - 1, chunks.bit_length() - 1
    others = list(range(low)) + list(range(low + 1, high))
    pairs = [others[i : i + 2] for i in range(0, len(others), 2)]

    core = 1 << low
    outer_bits = list(range(high, devices.bit_length() - 1))

    def masks(bits, straight=()):
        plain = [sum((i >> j & 1) << bit for j, bit in enumerate(bits)) for i in range(1 << len(bits))]
        if bits is outer_bits:
            return [mask ^ core * (i.bit_count() % 2) for i, mask in enumerate(plain)]
        return [mask if mask in (0, core) or mask in straight else mask ^ core for mask in plain]

    def order_of(straight=()):
        order = [0]
        for bits in reversed([[low]] + pairs):
            order = [mask ^ place for mask in masks(bits, straight) for place in order]
        return order

    straight = (1,) if blocks == 2 else ()
    order, gather_order = order_of(straight), order_of()
    way_bits = [sum(1 << bit - low - 1 for bit in bits if bit > low) for bits in pairs]
    parities = [
        (sum(bool(chip & bits) for bits in way_bits) + (chip >> high - low - 1).bit_count()) % 2
        for chip in range(groups // 2)
    ]

    def swap(value, mask):
        return lax.ppermute(value, both, [(i, i ^ mask) for i in range(devices)]) if mask else value

    far = jnp.stack([shift(features, -step) for step in range(1, blocks)])
    own, give, chosen = kernel(
        gather_kernel,
        "gather",
        (
            array((groups // 2, per_peer, width), F32),
            array((groups // 2, per_peer, width), F32),
            array((rows, slots), BF16),
        ),
        (send_count, send_index, features),
        spec=HBM,
        scratch=(
            pltpu.VMEM(send_count.shape, jnp.int32),
            pltpu.VMEM(send_index.shape, jnp.int32),
            pltpu.VMEM(features.shape, F32),
            pltpu.VMEM((slots, width), F32),
            pltpu.SemaphoreType.DMA((3,)),
        ),
        flops=work,
        traffic=4 * (rows + slots) * width,
    )
    got = swap(give, 1 << low)
    packed = jnp.stack([own, got], axis=1)
    arrived = [swap(packed[mask], 2 * mask + 1 << low) for mask in range(1, groups // 2)]
    arrival = list(range(groups // 2 - 1))
    arrival.append(arrival.pop(groups // 4 - 1))
    local, cross, tile_parts, weight_parts = kernel(
        prepare_kernel,
        "prepare",
        (
            array((rows, width), F32),
            array((2, rows, slots), BF16),
            array((blocks, 2, rows, rows), BF16),
            array((2, width, width), BF16),
        ),
        (features, far, tiles, weight, cross_dst, cross_weight),
        flops=3 * work,
        traffic=4 * (4 * rows + width) * width,
    )
    aligned = share % 8 == 0
    half = width // 2
    held = array((slots // 2 + (half if aligned else 0), width), F32)
    value, spread, keep, give, *partial = kernel(
        functools.partial(layer_kernel, order, parities, arrival),
        "layer",
        (array((rows, width), F32), array((2, rows, width), BF16), held, held)
        + (() if aligned else (array((width, width), F32),)),
        (local, cross, weight_parts, cotangent, own, got, *(arrived[i] for i in arrival)),
        scratch=(pltpu.VMEM((slots, width), F32), pltpu.VMEM((width, width), F32)),
        flops=15 * work,
        traffic=4 * (4 * rows + 2 * slots) * width,
    )
    if not aligned:
        ordered = partial[0].reshape(chunks, share, width)[chunk_number(chunks) ^ jnp.array(order)]
        keep = jnp.concatenate([ordered[: chunks // 2].reshape(half, width), keep])
        give = jnp.concatenate([ordered[chunks // 2 :].reshape(half, width), give])
    inner, leaving, output = kernel(
        inner_kernel,
        "inner",
        (array((rows, width), F32), array((blocks - 1, rows, width), F32), array((rows, width), F32)),
        (tile_parts, spread, value),
        flops=3 * work,
        traffic=4 * 6 * rows * width,
    )

    arrays = [keep, give, swap(give, 1 << low)]
    terms = [[(0, i * share, share), (2, i * share, share)] for i in range(chunks // 2)]
    moving = {
        2 * m + parities[m]: [(k, (2 * k, half + m * per_peer, per_peer)) for k in range(2)]
        for m in range(groups // 2)
    }
    far_pieces = []

    def pack(name, layout, scale=None):
        used = sorted({leaf[0] for pieces in layout for leaf in leaves(pieces)})
        layout = [[renumber(piece, used) for piece in pieces] for pieces in layout]
        out = tuple(array((sum(map(rows_of, pieces)), width), F32) for pieces in layout)
        operands = [arrays[i] for i in used]
        traffic = 8 * width * sum(o.shape[0] for o in out)
        return kernel(functools.partial(pack_kernel, layout, scale, len(used)), name, out, operands, traffic=traffic)

    for bits in pairs + [outer_bits]:
        last = bits is outer_bits
        keeps = len(terms) if last else len(terms) >> len(bits)
        layout, riders = [], []
        partners = list(enumerate(masks(bits, straight)))[:0:-1]
        if last:
            partners.sort(key=lambda partner: (2, 1, 3).index(partner[0]))
        for i, mask in partners:
            pieces = list(terms) if last else terms[i * keeps : (i + 1) * keeps]
            way, across = mask >> low, mask & (core - 1)
            all_ways = sum(1 << bit for bit in bits) >> low
            going = [q for q in sorted(moving) if not across and q & all_ways == way & all_ways]
            riders.append([(q, come) for q in going for come, _ in moving[q]])
            pieces += [piece for q in going for _, piece in moving[q]]
            if blocks == 2 and mask == 1:
                arrays.append(leaving[0])
                pieces.append((len(arrays) - 1, 0, rows))
            layout.append(pieces)
        sent = pack("pack", layout)
        came = {}
        for (i, mask), value, rides in zip(partners, sent, riders):
            arrays.append(swap(value, mask))
            number, first = len(arrays) - 1, 0
            came[i] = [(number, j * share, share) for j in range(keeps)]
            first = keeps * share
            for q, come in rides:
                way = mask >> low
                moving.setdefault(q ^ way, []).append((come ^ way, (number, first, per_peer)))
                first += per_peer
            if blocks == 2 and mask == 1:
                far_pieces.append((number, first, rows))
            for q in {q for q, _ in rides}:
                del moving[q]
        terms = [[terms[j]] + [came[i][j] for i in sorted(came)] for j in range(keeps)]
    if blocks > 2:
        for step in range(1, blocks):
            arrays.append(shift(leaving[step - 1], step))
            far_pieces.append((len(arrays) - 1, 0, rows))

    sums = pack("sum", [terms], nodes ** (-0.5))[0].reshape(1, share, width)
    for bits in reversed(pairs):
        sums = jnp.concatenate([swap(sums, mask) for mask in masks(bits)])
    other = swap(sums, 1 << low)
    if aligned:
        grad_weight = kernel(
            functools.partial(place_kernel, gather_order),
            "place",
            array((width, width), F32),
            (sums, other),
            traffic=8 * width * width,
        )
    else:
        places = jnp.array([gather_order.index(i) for i in range(chunks)])[chunk_number(chunks) ^ jnp.arange(chunks)]
        grad_weight = jnp.concatenate([sums, other])[places].reshape(width, width)

    came = moving[0]
    used = sorted({piece[0] for _, piece in came} | {piece[0] for piece in far_pieces})
    grad_features = kernel(
        functools.partial(
            finish_kernel,
            [(distance, renumber(piece, used)) for distance, piece in came],
            [renumber(piece, used) for piece in far_pieces],
        ),
        "finish",
        array((rows, width), F32),
        (chosen, inner, *(arrays[i] for i in used)),
        scratch=(pltpu.VMEM((slots, width), F32),),
        flops=2 * work,
        traffic=4 * (3 * rows + slots) * width,
    )
    return (output, grad_features, grad_weight)


def solution(mesh):
    return jax.shard_map(
        body,
        mesh=mesh,
        in_specs=(
            P(("comm", "blk"), None),
            P(("comm", "blk"), None),
            P(),
            P(("comm", "blk"), None),
            P(("comm", "blk"), None),
            P(("comm", "blk"), None),
            P(("comm", "blk"), None),
            P(("comm", "blk"), None),
        ),
        out_specs=(P(("comm", "blk"), None), P(("comm", "blk"), None), P()),
        check_vma=False,
    )
```

```python
import functools
import math

import jax
import jax.numpy as jnp
from jax import lax
from jax.experimental import pallas as pl
from jax.experimental.pallas import tpu as pltpu
from jax.sharding import PartitionSpec as P

F32 = jnp.float32
BF16 = jnp.bfloat16
VMEM = pl.BlockSpec(memory_space=pltpu.VMEM)
HBM = pl.BlockSpec(memory_space=pltpu.HBM)


def split(value):
    high = value.astype(BF16)
    return high, (value - high.astype(F32)).astype(BF16)


def product(a, b, dims):
    return lax.dot_general(a, b, (dims, ((), ())), preferred_element_type=F32)


def dot3(a, b, dims=((1,), (0,))):
    (a_high, a_low), (b_high, b_low) = a, b
    left = jnp.concatenate([a_low, a_high, a_high], axis=dims[0][0])
    right = jnp.concatenate([b_high, b_low, b_high], axis=dims[1][0])
    return product(left, right, dims)


def dot_onehot(a, b, dims):
    left = jnp.concatenate([a, a], axis=dims[0][0])
    return product(left, jnp.concatenate([b[1], b[0]], axis=dims[1][0]), dims)


def tree(terms):
    while len(terms) > 1:
        terms = [terms[i] + terms[i + 1] for i in range(0, len(terms), 2)]
    return terms[0]


def send_matrix(counts, index, rows):
    groups, slots = counts.shape[1], index.shape[1]
    per_peer = slots // groups
    lane = lax.broadcasted_iota(jnp.int32, (groups, slots), 1)
    first = lax.broadcasted_iota(jnp.int32, (groups, slots), 0) * per_peer
    of_peer = ((lane >= first) & (lane < first + per_peer)).astype(F32)
    limit = jnp.dot(counts.astype(F32), of_peer, preferred_element_type=F32)
    place = lax.broadcasted_iota(jnp.int32, (1, slots), 1) % per_peer
    chosen = jnp.where(place.astype(F32) < limit, index, -1)
    return (lax.broadcasted_iota(jnp.int32, (rows, slots), 0) == chosen).astype(F32).astype(BF16)


def gather_kernel(
    count_hbm, index_hbm, features_hbm, own_ref, give_ref, chosen_ref, count_ref, index_ref, features_ref, rows_ref, sems
):
    pairs = ((count_hbm, count_ref), (index_hbm, index_ref), (features_hbm, features_ref))
    copies = [pltpu.make_async_copy(source, target, sems.at[i]) for i, (source, target) in enumerate(pairs)]
    for copy in copies:
        copy.start()
    copies[0].wait()
    copies[1].wait()
    chosen = send_matrix(count_ref[...], index_ref[...], features_ref.shape[0])
    chosen_ref[...] = chosen
    copies[2].wait()
    rows_ref[...] = dot_onehot(chosen, split(features_ref[...]), ((0,), (0,)))
    me = lax.axis_index("comm")
    chips, per_peer = own_ref.shape[:2]
    for mask in range(chips):
        for k, out_ref in enumerate((own_ref, give_ref)):
            start = lax.bitwise_xor(me, 2 * mask + (k ^ (mask > 0))) * per_peer
            out_ref[mask] = rows_ref[pl.ds(pl.multiple_of(start, per_peer), per_peer), :]


def prepare_kernel(
    near_ref, far_ref, tiles_ref, weight_ref, target_ref, edge_ref,
    local_ref, cross_ref, tiles_out, weight_out,
):
    rows = near_ref.shape[0]
    blocks = far_ref.shape[0] + 1
    slots = target_ref.shape[1]
    me = lax.axis_index("blk")

    total = None
    for step in range(blocks):
        start = lax.rem(me + step, blocks) * rows
        tile = split(tiles_ref[:, pl.ds(pl.multiple_of(start, rows), rows)])
        tiles_out[step, 0], tiles_out[step, 1] = tile
        term = dot3(tile, split(near_ref[...] if step == 0 else far_ref[step - 1]))
        total = term if total is None else total + term
    local_ref[...] = total
    hit = lax.broadcasted_iota(jnp.int32, (rows, slots), 0) == target_ref[...]
    cross_ref[0], cross_ref[1] = split(jnp.where(hit, edge_ref[...], 0.0))
    weight_out[0], weight_out[1] = split(weight_ref[...])


def chunk_number(chunks):
    blocks = lax.axis_size("blk")
    number = lax.axis_index("comm") * blocks + lax.axis_index("blk")
    outer = lax.div(number, chunks)
    crossed = lax.rem(outer + lax.div(outer, 2), 2) * blocks
    return lax.bitwise_xor(lax.rem(number, chunks), crossed)


def layer_kernel(
    order, parities, arrival, local_ref, cross_ref, weight_ref, cotangent_ref, own_ref, got_ref, *refs
):
    chips, per_peer = own_ref.shape[:2]
    arrived_refs, refs = refs[: chips - 1], refs[chips - 1 :]
    out_ref, spread_ref, keep_ref, give_ref, *partial_refs, slots_ref, terms_ref = refs
    peer = lax.axis_index("comm")
    for mask in range(chips):
        for k in range(2):
            start = lax.bitwise_xor(peer, 2 * mask + (k ^ (mask > 0))) * per_peer
            block = arrived_refs[arrival.index(mask - 1)][k] if mask else (got_ref if k else own_ref)[0]
            slots_ref[pl.ds(pl.multiple_of(start, per_peer), per_peer), :] = block
    cross = cross_ref[0], cross_ref[1]
    weight = weight_ref[0], weight_ref[1]

    aggregated = split(local_ref[...] + dot3(cross, split(slots_ref[...])))
    pre = dot3(aggregated, weight)
    cdf = 0.5 * (1.0 + lax.erf(pre * math.sqrt(0.5)))
    density = jnp.exp(-0.5 * pre * pre) * (1.0 / math.sqrt(2.0 * math.pi))
    grad_pre = split(cotangent_ref[...] * (cdf + pre * density))
    out_ref[...] = pre * cdf
    terms_ref[...] = dot3(aggregated, grad_pre, ((0,), (0,)))
    spread = split(dot3(grad_pre, weight, ((1,), (1,))))
    spread_ref[0], spread_ref[1] = spread
    slots_ref[...] = dot3(cross, spread, ((0,), (0,)))

    half = 0
    if partial_refs:
        partial_refs[0][...] = terms_ref[...]
    else:
        half = terms_ref.shape[0] // 2
        share = terms_ref.shape[0] // len(order)
        me = chunk_number(len(order))
        for place, relative in enumerate(order):
            start = lax.bitwise_xor(me, relative) * share
            chunk = terms_ref[pl.ds(pl.multiple_of(start, share), share), :]
            target_ref = keep_ref if place < len(order) // 2 else give_ref
            target_ref[pl.ds(place * share % half, share), :] = chunk
    for mask in range(chips):
        for k, target_ref in enumerate((keep_ref, give_ref)):
            start = lax.bitwise_xor(peer, 2 * mask + (k ^ parities[mask])) * per_peer
            block = slots_ref[pl.ds(pl.multiple_of(start, per_peer), per_peer), :]
            target_ref[pl.ds(half + mask * per_peer, per_peer), :] = block


def place_kernel(order, mine_ref, other_ref, out_ref):
    half, share = mine_ref.shape[:2]
    me = chunk_number(len(order))
    for i, relative in enumerate(order):
        start = lax.bitwise_xor(me, relative) * share
        out_ref[pl.ds(pl.multiple_of(start, share), share), :] = mine_ref[i] if i < half else other_ref[i - half]


def inner_kernel(tiles_ref, spread_ref, value_ref, near_ref, far_ref, out_ref):
    spread = spread_ref[0], spread_ref[1]
    for step in range(far_ref.shape[0]):
        far_ref[step] = dot3((tiles_ref[step + 1, 0], tiles_ref[step + 1, 1]), spread, ((0,), (0,)))
    near_ref[...] = dot3((tiles_ref[0, 0], tiles_ref[0, 1]), spread, ((0,), (0,)))
    out_ref[...] = value_ref[...]


def value_of(piece, refs):
    if isinstance(piece, list):
        return tree([value_of(term, refs) for term in piece])
    source, first, rows = piece
    return refs[source][first : first + rows, :]


def rows_of(piece):
    return rows_of(piece[0]) if isinstance(piece, list) else piece[2]


def leaves(piece):
    return [leaf for term in piece for leaf in leaves(term)] if isinstance(piece, list) else [piece]


def renumber(piece, used):
    if isinstance(piece, list):
        return [renumber(term, used) for term in piece]
    return (used.index(piece[0]), *piece[1:])


def pack_kernel(layout, scale, count, *refs):
    for pieces, out_ref in zip(layout, refs[count:]):
        first = 0
        for piece in pieces:
            rows = rows_of(piece)
            value = value_of(piece, refs)
            out_ref[first : first + rows, :] = value if scale is None else value * scale
            first += rows


def finish_kernel(blocks, far, chosen_ref, near_ref, *refs):
    *refs, grad_ref, slots_ref = refs
    peer = lax.axis_index("comm")
    for distance, piece in blocks:
        rows = piece[2]
        start = lax.bitwise_xor(peer, distance) * rows
        slots_ref[pl.ds(pl.multiple_of(start, rows), rows), :] = value_of(piece, refs)
    total = near_ref[...]
    for piece in far:
        total += value_of(piece, refs)
    grad_ref[...] = total + dot_onehot(chosen_ref[...], split(slots_ref[...]), ((1,), (0,)))


def kernel(body, name, out, operands, spec=VMEM, scratch=(), flops=0, traffic=0, after=()):
    count = len(operands)
    if spec is HBM:
        operands = [pltpu.with_memory_space_constraint(x, pltpu.HBM) for x in operands]
    return pl.pallas_call(
        lambda *refs: body(*refs[:count], *refs[count + len(after) :]),
        out_shape=out,
        in_specs=[spec] * count + [pl.BlockSpec(memory_space=pl.ANY)] * len(after),
        out_specs=jax.tree.map(lambda _: VMEM, out),
        scratch_shapes=list(scratch),
        compiler_params=pltpu.CompilerParams(vmem_limit_bytes=16 * 1024 * 1024),
        cost_estimate=pl.CostEstimate(flops=flops, bytes_accessed=traffic, transcendentals=0),
        name=name,
    )(*operands, *after)


def body(features, tiles, weight, cotangent, send_count, send_index, cross_dst, cross_weight):
    rows, width = features.shape
    groups = lax.axis_size("comm")
    blocks = lax.axis_size("blk")
    slots = send_index.shape[1]
    per_peer = slots // groups
    nodes = rows * groups * blocks
    array = jax.ShapeDtypeStruct
    work = 2 * rows * slots * width

    def shift(value, step):
        pairs = [(i, (i + step) % blocks) for i in range(blocks)]
        return lax.ppermute(value, "blk", pairs)

    def exchange(value):
        return lax.all_to_all(value, "comm", split_axis=0, concat_axis=0, tiled=True)

    both = ("comm", "blk")
    devices = groups * blocks
    outer = min(4, groups // 2)
    chunks = devices // outer
    share = width // chunks
    low, high = blocks.bit_length() - 1, chunks.bit_length() - 1
    others = list(range(low)) + list(range(low + 1, high))
    pairs = [others[i : i + 2] for i in range(0, len(others), 2)]

    core = 1 << low
    outer_bits = list(range(high, devices.bit_length() - 1))

    def masks(bits, straight=()):
        plain = [sum((i >> j & 1) << bit for j, bit in enumerate(bits)) for i in range(1 << len(bits))]
        if bits is outer_bits:
            return [mask ^ core * (i.bit_count() % 2) for i, mask in enumerate(plain)]
        return [mask if mask in (0, core) or mask in straight else mask ^ core for mask in plain]

    def order_of(straight=()):
        order = [0]
        for bits in reversed([[low]] + pairs):
            order = [mask ^ place for mask in masks(bits, straight) for place in order]
        return order

    straight = (1,) if blocks == 2 else ()
    order, gather_order = order_of(straight), order_of()
    way_bits = [sum(1 << bit - low - 1 for bit in bits if bit > low) for bits in pairs]
    parities = [
        (sum(bool(chip & bits) for bits in way_bits) + (chip >> high - low - 1).bit_count()) % 2
        for chip in range(groups // 2)
    ]

    def swap(value, mask):
        return lax.ppermute(value, both, [(i, i ^ mask) for i in range(devices)]) if mask else value

    far = jnp.stack([shift(features, -step) for step in range(1, blocks)])
    own, give, chosen = kernel(
        gather_kernel,
        "gather",
        (
            array((groups // 2, per_peer, width), F32),
            array((groups // 2, per_peer, width), F32),
            array((rows, slots), BF16),
        ),
        (send_count, send_index, features),
        spec=HBM,
        scratch=(
            pltpu.VMEM(send_count.shape, jnp.int32),
            pltpu.VMEM(send_index.shape, jnp.int32),
            pltpu.VMEM(features.shape, F32),
            pltpu.VMEM((slots, width), F32),
            pltpu.SemaphoreType.DMA((3,)),
        ),
        flops=work,
        traffic=4 * (rows + slots) * width,
    )
    got = swap(give, 1 << low)
    packed = jnp.stack([own, got], axis=1)
    arrived = [swap(packed[mask], 2 * mask + 1 << low) for mask in range(1, groups // 2)]
    arrival = list(range(groups // 2 - 1))
    arrival.append(arrival.pop(groups // 4 - 1))
    local, cross, tile_parts, weight_parts = kernel(
        prepare_kernel,
        "prepare",
        (
            array((rows, width), F32),
            array((2, rows, slots), BF16),
            array((blocks, 2, rows, rows), BF16),
            array((2, width, width), BF16),
        ),
        (features, far, tiles, weight, cross_dst, cross_weight),
        flops=3 * work,
        traffic=4 * (4 * rows + width) * width,
    )
    aligned = share % 8 == 0
    half = width // 2
    held = array((slots // 2 + (half if aligned else 0), width), F32)
    value, spread, keep, give, *partial = kernel(
        functools.partial(layer_kernel, order, parities, arrival),
        "layer",
        (array((rows, width), F32), array((2, rows, width), BF16), held, held)
        + (() if aligned else (array((width, width), F32),)),
        (local, cross, weight_parts, cotangent, own, got, *(arrived[i] for i in arrival)),
        scratch=(pltpu.VMEM((slots, width), F32), pltpu.VMEM((width, width), F32)),
        flops=15 * work,
        traffic=4 * (4 * rows + 2 * slots) * width,
    )
    if not aligned:
        ordered = partial[0].reshape(chunks, share, width)[chunk_number(chunks) ^ jnp.array(order)]
        keep = jnp.concatenate([ordered[: chunks // 2].reshape(half, width), keep])
        give = jnp.concatenate([ordered[chunks // 2 :].reshape(half, width), give])
    inner, leaving, output = kernel(
        inner_kernel,
        "inner",
        (array((rows, width), F32), array((blocks - 1, rows, width), F32), array((rows, width), F32)),
        (tile_parts, spread, value),
        flops=3 * work,
        traffic=4 * 6 * rows * width,
    )

    arrays = [keep, give, swap(give, 1 << low)]
    terms = [[(0, i * share, share), (2, i * share, share)] for i in range(chunks // 2)]
    moving = {
        2 * m + parities[m]: [(k, (2 * k, half + m * per_peer, per_peer)) for k in range(2)]
        for m in range(groups // 2)
    }
    far_pieces = []

    def pack(name, layout, scale=None):
        used = sorted({leaf[0] for pieces in layout for leaf in leaves(pieces)})
        layout = [[renumber(piece, used) for piece in pieces] for pieces in layout]
        out = tuple(array((sum(map(rows_of, pieces)), width), F32) for pieces in layout)
        operands = [arrays[i] for i in used]
        traffic = 8 * width * sum(o.shape[0] for o in out)
        return kernel(functools.partial(pack_kernel, layout, scale, len(used)), name, out, operands, traffic=traffic)

    for bits in pairs + [outer_bits]:
        last = bits is outer_bits
        keeps = len(terms) if last else len(terms) >> len(bits)
        layout, riders = [], []
        partners = list(enumerate(masks(bits, straight)))[:0:-1]
        if last:
            partners.sort(key=lambda partner: partner[0] != 2)
        for i, mask in partners:
            pieces = list(terms) if last else terms[i * keeps : (i + 1) * keeps]
            way, across = mask >> low, mask & (core - 1)
            all_ways = sum(1 << bit for bit in bits) >> low
            going = [q for q in sorted(moving) if not across and q & all_ways == way & all_ways]
            riders.append([(q, come) for q in going for come, _ in moving[q]])
            pieces += [piece for q in going for _, piece in moving[q]]
            if blocks == 2 and mask == 1:
                arrays.append(leaving[0])
                pieces.append((len(arrays) - 1, 0, rows))
            layout.append(pieces)
        sent = pack("pack", layout)
        came = {}
        for (i, mask), value, rides in zip(partners, sent, riders):
            arrays.append(swap(value, mask))
            number, first = len(arrays) - 1, 0
            came[i] = [(number, j * share, share) for j in range(keeps)]
            first = keeps * share
            for q, come in rides:
                way = mask >> low
                moving.setdefault(q ^ way, []).append((come ^ way, (number, first, per_peer)))
                first += per_peer
            if blocks == 2 and mask == 1:
                far_pieces.append((number, first, rows))
            for q in {q for q, _ in rides}:
                del moving[q]
        terms = [[terms[j]] + [came[i][j] for i in sorted(came)] for j in range(keeps)]
    if blocks > 2:
        for step in range(1, blocks):
            arrays.append(shift(leaving[step - 1], step))
            far_pieces.append((len(arrays) - 1, 0, rows))

    sums = pack("sum", [terms], nodes ** (-0.5))[0].reshape(1, share, width)
    for bits in reversed(pairs):
        sums = jnp.concatenate([swap(sums, mask) for mask in masks(bits)])
    other = swap(sums, 1 << low)
    if aligned:
        grad_weight = kernel(
            functools.partial(place_kernel, gather_order),
            "place",
            array((width, width), F32),
            (sums, other),
            traffic=8 * width * width,
        )
    else:
        places = jnp.array([gather_order.index(i) for i in range(chunks)])[chunk_number(chunks) ^ jnp.arange(chunks)]
        grad_weight = jnp.concatenate([sums, other])[places].reshape(width, width)

    came = moving[0]
    used = sorted({piece[0] for _, piece in came} | {piece[0] for piece in far_pieces})
    grad_features = kernel(
        functools.partial(
            finish_kernel,
            [(distance, renumber(piece, used)) for distance, piece in came],
            [renumber(piece, used) for piece in far_pieces],
        ),
        "finish",
        array((rows, width), F32),
        (chosen, inner, *(arrays[i] for i in used)),
        scratch=(pltpu.VMEM((slots, width), F32),),
        flops=2 * work,
        traffic=4 * (3 * rows + slots) * width,
    )
    return (output, grad_features, grad_weight)


def solution(mesh):
    return jax.shard_map(
        body,
        mesh=mesh,
        in_specs=(
            P(("comm", "blk"), None),
            P(("comm", "blk"), None),
            P(),
            P(("comm", "blk"), None),
            P(("comm", "blk"), None),
            P(("comm", "blk"), None),
            P(("comm", "blk"), None),
            P(("comm", "blk"), None),
        ),
        out_specs=(P(("comm", "blk"), None), P(("comm", "blk"), None), P()),
        check_vma=False,
    )
```

```python
import functools
import math

import jax
import jax.numpy as jnp
from jax import lax
from jax.experimental import pallas as pl
from jax.experimental.pallas import tpu as pltpu
from jax.sharding import PartitionSpec as P

F32 = jnp.float32
BF16 = jnp.bfloat16
VMEM = pl.BlockSpec(memory_space=pltpu.VMEM)
HBM = pl.BlockSpec(memory_space=pltpu.HBM)


def split(value):
    high = value.astype(BF16)
    return high, (value - high.astype(F32)).astype(BF16)


def product(a, b, dims):
    return lax.dot_general(a, b, (dims, ((), ())), preferred_element_type=F32)


def dot3(a, b, dims=((1,), (0,))):
    (a_high, a_low), (b_high, b_low) = a, b
    left = jnp.concatenate([a_low, a_high, a_high], axis=dims[0][0])
    right = jnp.concatenate([b_high, b_low, b_high], axis=dims[1][0])
    return product(left, right, dims)


def dot_onehot(a, b, dims):
    left = jnp.concatenate([a, a], axis=dims[0][0])
    return product(left, jnp.concatenate([b[1], b[0]], axis=dims[1][0]), dims)


def tree(terms):
    while len(terms) > 1:
        terms = [terms[i] + terms[i + 1] for i in range(0, len(terms), 2)]
    return terms[0]


def send_matrix(counts, index, rows):
    groups, slots = counts.shape[1], index.shape[1]
    per_peer = slots // groups
    lane = lax.broadcasted_iota(jnp.int32, (groups, slots), 1)
    first = lax.broadcasted_iota(jnp.int32, (groups, slots), 0) * per_peer
    of_peer = ((lane >= first) & (lane < first + per_peer)).astype(F32)
    limit = jnp.dot(counts.astype(F32), of_peer, preferred_element_type=F32)
    place = lax.broadcasted_iota(jnp.int32, (1, slots), 1) % per_peer
    chosen = jnp.where(place.astype(F32) < limit, index, -1)
    return (lax.broadcasted_iota(jnp.int32, (rows, slots), 0) == chosen).astype(F32).astype(BF16)


def gather_kernel(
    count_hbm, index_hbm, features_hbm, own_ref, give_ref, chosen_ref, count_ref, index_ref, features_ref, rows_ref, sems
):
    pairs = ((count_hbm, count_ref), (index_hbm, index_ref), (features_hbm, features_ref))
    copies = [pltpu.make_async_copy(source, target, sems.at[i]) for i, (source, target) in enumerate(pairs)]
    for copy in copies:
        copy.start()
    copies[0].wait()
    copies[1].wait()
    chosen = send_matrix(count_ref[...], index_ref[...], features_ref.shape[0])
    chosen_ref[...] = chosen
    copies[2].wait()
    rows_ref[...] = dot_onehot(chosen, split(features_ref[...]), ((0,), (0,)))
    me = lax.axis_index("comm")
    chips, per_peer = own_ref.shape[:2]
    for mask in range(chips):
        for k, out_ref in enumerate((own_ref, give_ref)):
            start = lax.bitwise_xor(me, 2 * mask + (k ^ (mask > 0))) * per_peer
            out_ref[mask] = rows_ref[pl.ds(pl.multiple_of(start, per_peer), per_peer), :]


def prepare_kernel(
    near_ref, far_ref, tiles_ref, weight_ref, target_ref, edge_ref,
    local_ref, cross_ref, tiles_out, weight_out,
):
    rows = near_ref.shape[0]
    blocks = far_ref.shape[0] + 1
    slots = target_ref.shape[1]
    me = lax.axis_index("blk")

    total = None
    for step in range(blocks):
        start = lax.rem(me + step, blocks) * rows
        tile = split(tiles_ref[:, pl.ds(pl.multiple_of(start, rows), rows)])
        tiles_out[step, 0], tiles_out[step, 1] = tile
        term = dot3(tile, split(near_ref[...] if step == 0 else far_ref[step - 1]))
        total = term if total is None else total + term
    local_ref[...] = total
    hit = lax.broadcasted_iota(jnp.int32, (rows, slots), 0) == target_ref[...]
    cross_ref[0], cross_ref[1] = split(jnp.where(hit, edge_ref[...], 0.0))
    weight_out[0], weight_out[1] = split(weight_ref[...])


def chunk_number(chunks):
    blocks = lax.axis_size("blk")
    number = lax.axis_index("comm") * blocks + lax.axis_index("blk")
    outer = lax.div(number, chunks)
    crossed = lax.rem(outer + lax.div(outer, 2), 2) * blocks
    return lax.bitwise_xor(lax.rem(number, chunks), crossed)


def layer_kernel(
    order, parities, arrival, local_ref, cross_ref, weight_ref, cotangent_ref, own_ref, got_ref, *refs
):
    chips, per_peer = own_ref.shape[:2]
    arrived_refs, refs = refs[: chips - 1], refs[chips - 1 :]
    out_ref, spread_ref, keep_ref, give_ref, *partial_refs, slots_ref, terms_ref = refs
    peer = lax.axis_index("comm")
    for mask in range(chips):
        for k in range(2):
            start = lax.bitwise_xor(peer, 2 * mask + (k ^ (mask > 0))) * per_peer
            block = arrived_refs[arrival.index(mask - 1)][k] if mask else (got_ref if k else own_ref)[0]
            slots_ref[pl.ds(pl.multiple_of(start, per_peer), per_peer), :] = block
    cross = cross_ref[0], cross_ref[1]
    weight = weight_ref[0], weight_ref[1]

    aggregated = split(local_ref[...] + dot3(cross, split(slots_ref[...])))
    pre = dot3(aggregated, weight)
    cdf = 0.5 * (1.0 + lax.erf(pre * math.sqrt(0.5)))
    density = jnp.exp(-0.5 * pre * pre) * (1.0 / math.sqrt(2.0 * math.pi))
    grad_pre = split(cotangent_ref[...] * (cdf + pre * density))
    out_ref[...] = pre * cdf
    terms_ref[...] = dot3(aggregated, grad_pre, ((0,), (0,)))
    spread = split(dot3(grad_pre, weight, ((1,), (1,))))
    spread_ref[0], spread_ref[1] = spread
    slots_ref[...] = dot3(cross, spread, ((0,), (0,)))

    half = 0
    if partial_refs:
        partial_refs[0][...] = terms_ref[...]
    else:
        half = terms_ref.shape[0] // 2
        share = terms_ref.shape[0] // len(order)
        me = chunk_number(len(order))
        for place, relative in enumerate(order):
            start = lax.bitwise_xor(me, relative) * share
            chunk = terms_ref[pl.ds(pl.multiple_of(start, share), share), :]
            target_ref = keep_ref if place < len(order) // 2 else give_ref
            target_ref[pl.ds(place * share % half, share), :] = chunk
    for mask in range(chips):
        for k, target_ref in enumerate((keep_ref, give_ref)):
            start = lax.bitwise_xor(peer, 2 * mask + (k ^ parities[mask])) * per_peer
            block = slots_ref[pl.ds(pl.multiple_of(start, per_peer), per_peer), :]
            target_ref[pl.ds(half + mask * per_peer, per_peer), :] = block


def place_kernel(order, mine_ref, other_ref, out_ref):
    half, share = mine_ref.shape[:2]
    me = chunk_number(len(order))
    for i, relative in enumerate(order):
        start = lax.bitwise_xor(me, relative) * share
        out_ref[pl.ds(pl.multiple_of(start, share), share), :] = mine_ref[i] if i < half else other_ref[i - half]


def inner_kernel(tiles_ref, spread_ref, value_ref, near_ref, far_ref, out_ref):
    spread = spread_ref[0], spread_ref[1]
    for step in range(far_ref.shape[0]):
        far_ref[step] = dot3((tiles_ref[step + 1, 0], tiles_ref[step + 1, 1]), spread, ((0,), (0,)))
    near_ref[...] = dot3((tiles_ref[0, 0], tiles_ref[0, 1]), spread, ((0,), (0,)))
    out_ref[...] = value_ref[...]


def value_of(piece, refs):
    if isinstance(piece, list):
        return tree([value_of(term, refs) for term in piece])
    source, first, rows = piece
    return refs[source][first : first + rows, :]


def rows_of(piece):
    return rows_of(piece[0]) if isinstance(piece, list) else piece[2]


def leaves(piece):
    return [leaf for term in piece for leaf in leaves(term)] if isinstance(piece, list) else [piece]


def renumber(piece, used):
    if isinstance(piece, list):
        return [renumber(term, used) for term in piece]
    return (used.index(piece[0]), *piece[1:])


def pack_kernel(layout, scale, count, *refs):
    for pieces, out_ref in zip(layout, refs[count:]):
        first = 0
        for piece in pieces:
            rows = rows_of(piece)
            value = value_of(piece, refs)
            out_ref[first : first + rows, :] = value if scale is None else value * scale
            first += rows


def finish_kernel(blocks, far, chosen_ref, near_ref, *refs):
    *refs, grad_ref, slots_ref = refs
    peer = lax.axis_index("comm")
    for distance, piece in blocks:
        rows = piece[2]
        start = lax.bitwise_xor(peer, distance) * rows
        slots_ref[pl.ds(pl.multiple_of(start, rows), rows), :] = value_of(piece, refs)
    total = near_ref[...]
    for piece in far:
        total += value_of(piece, refs)
    grad_ref[...] = total + dot_onehot(chosen_ref[...], split(slots_ref[...]), ((1,), (0,)))


def kernel(body, name, out, operands, spec=VMEM, scratch=(), flops=0, traffic=0, after=()):
    count = len(operands)
    if spec is HBM:
        operands = [pltpu.with_memory_space_constraint(x, pltpu.HBM) for x in operands]
    return pl.pallas_call(
        lambda *refs: body(*refs[:count], *refs[count + len(after) :]),
        out_shape=out,
        in_specs=[spec] * count + [pl.BlockSpec(memory_space=pl.ANY)] * len(after),
        out_specs=jax.tree.map(lambda _: VMEM, out),
        scratch_shapes=list(scratch),
        compiler_params=pltpu.CompilerParams(vmem_limit_bytes=16 * 1024 * 1024),
        cost_estimate=pl.CostEstimate(flops=flops, bytes_accessed=traffic, transcendentals=0),
        name=name,
    )(*operands, *after)


def body(features, tiles, weight, cotangent, send_count, send_index, cross_dst, cross_weight):
    rows, width = features.shape
    groups = lax.axis_size("comm")
    blocks = lax.axis_size("blk")
    slots = send_index.shape[1]
    per_peer = slots // groups
    nodes = rows * groups * blocks
    array = jax.ShapeDtypeStruct
    work = 2 * rows * slots * width

    def shift(value, step):
        pairs = [(i, (i + step) % blocks) for i in range(blocks)]
        return lax.ppermute(value, "blk", pairs)

    def exchange(value):
        return lax.all_to_all(value, "comm", split_axis=0, concat_axis=0, tiled=True)

    both = ("comm", "blk")
    devices = groups * blocks
    outer = min(4, groups // 2)
    chunks = devices // outer
    share = width // chunks
    low, high = blocks.bit_length() - 1, chunks.bit_length() - 1
    others = list(range(low)) + list(range(low + 1, high))
    pairs = [others[i : i + 2] for i in range(0, len(others), 2)]

    core = 1 << low
    outer_bits = list(range(high, devices.bit_length() - 1))

    def masks(bits):
        plain = [sum((i >> j & 1) << bit for j, bit in enumerate(bits)) for i in range(1 << len(bits))]
        if bits is outer_bits:
            return [mask ^ core * (i.bit_count() % 2) for i, mask in enumerate(plain)]
        return [mask if mask in (0, core) else mask ^ core for mask in plain]

    def order_of():
        order = [0]
        for bits in reversed([[low]] + pairs):
            order = [mask ^ place for mask in masks(bits) for place in order]
        return order

    order = order_of()
    way_bits = [sum(1 << bit - low - 1 for bit in bits if bit > low) for bits in pairs]
    parities = [
        (sum(bool(chip & bits) for bits in way_bits) + (chip >> high - low - 1).bit_count()) % 2
        for chip in range(groups // 2)
    ]

    def swap(value, mask):
        return lax.ppermute(value, both, [(i, i ^ mask) for i in range(devices)]) if mask else value

    far = jnp.stack([shift(features, -step) for step in range(1, blocks)])
    own, give, chosen = kernel(
        gather_kernel,
        "gather",
        (
            array((groups // 2, per_peer, width), F32),
            array((groups // 2, per_peer, width), F32),
            array((rows, slots), BF16),
        ),
        (send_count, send_index, features),
        spec=HBM,
        scratch=(
            pltpu.VMEM(send_count.shape, jnp.int32),
            pltpu.VMEM(send_index.shape, jnp.int32),
            pltpu.VMEM(features.shape, F32),
            pltpu.VMEM((slots, width), F32),
            pltpu.SemaphoreType.DMA((3,)),
        ),
        flops=work,
        traffic=4 * (rows + slots) * width,
    )
    got = swap(give, 1 << low)
    packed = jnp.stack([own, got], axis=1)
    arrived = [swap(packed[mask], 2 * mask + 1 << low) for mask in range(1, groups // 2)]
    arrival = list(range(groups // 2 - 1))
    arrival.append(arrival.pop(groups // 4 - 1))
    local, cross, tile_parts, weight_parts = kernel(
        prepare_kernel,
        "prepare",
        (
            array((rows, width), F32),
            array((2, rows, slots), BF16),
            array((blocks, 2, rows, rows), BF16),
            array((2, width, width), BF16),
        ),
        (features, far, tiles, weight, cross_dst, cross_weight),
        flops=3 * work,
        traffic=4 * (4 * rows + width) * width,
    )
    aligned = share % 8 == 0
    half = width // 2
    held = array((slots // 2 + (half if aligned else 0), width), F32)
    value, spread, keep, give, *partial = kernel(
        functools.partial(layer_kernel, order, parities, arrival),
        "layer",
        (array((rows, width), F32), array((2, rows, width), BF16), held, held)
        + (() if aligned else (array((width, width), F32),)),
        (local, cross, weight_parts, cotangent, own, got, *(arrived[i] for i in arrival)),
        scratch=(pltpu.VMEM((slots, width), F32), pltpu.VMEM((width, width), F32)),
        flops=15 * work,
        traffic=4 * (4 * rows + 2 * slots) * width,
    )
    if not aligned:
        ordered = partial[0].reshape(chunks, share, width)[chunk_number(chunks) ^ jnp.array(order)]
        keep = jnp.concatenate([ordered[: chunks // 2].reshape(half, width), keep])
        give = jnp.concatenate([ordered[chunks // 2 :].reshape(half, width), give])
    inner, leaving, output = kernel(
        inner_kernel,
        "inner",
        (array((rows, width), F32), array((blocks - 1, rows, width), F32), array((rows, width), F32)),
        (tile_parts, spread, value),
        flops=3 * work,
        traffic=4 * 6 * rows * width,
    )

    arrays = [keep, give, swap(give, 1 << low)]
    terms = [[(0, i * share, share), (2, i * share, share)] for i in range(chunks // 2)]
    moving = {
        2 * m + parities[m]: [(k, (2 * k, half + m * per_peer, per_peer)) for k in range(2)]
        for m in range(groups // 2)
    }
    far_pieces = []

    def pack(name, layout, scale=None, after=()):
        used = sorted({leaf[0] for pieces in layout for leaf in leaves(pieces)})
        layout = [[renumber(piece, used) for piece in pieces] for pieces in layout]
        out = tuple(array((sum(map(rows_of, pieces)), width), F32) for pieces in layout)
        operands = [arrays[i] for i in used]
        traffic = 8 * width * sum(o.shape[0] for o in out)
        return kernel(functools.partial(pack_kernel, layout, scale, len(used)), name, out, operands, traffic=traffic, after=after)

    for bits in pairs + [outer_bits]:
        last = bits is outer_bits
        keeps = len(terms) if last else len(terms) >> len(bits)
        layout, riders = [], []
        partners = list(enumerate(masks(bits)))[:0:-1]
        if last:
            partners.sort(key=lambda partner: partner[0] != 2)
        for i, mask in partners:
            pieces = list(terms) if last else terms[i * keeps : (i + 1) * keeps]
            way, across = mask >> low, mask & (core - 1)
            all_ways = sum(1 << bit for bit in bits) >> low
            going = [q for q in sorted(moving) if not across and q & all_ways == way & all_ways]
            riders.append([(q, come) for q in going for come, _ in moving[q]])
            pieces += [piece for q in going for _, piece in moving[q]]
            layout.append(pieces)
        sent = pack("pack", layout)
        came = {}
        for (i, mask), value, rides in zip(partners, sent, riders):
            arrays.append(swap(value, mask))
            number, first = len(arrays) - 1, 0
            came[i] = [(number, j * share, share) for j in range(keeps)]
            first = keeps * share
            for q, come in rides:
                way = mask >> low
                moving.setdefault(q ^ way, []).append((come ^ way, (number, first, per_peer)))
                first += per_peer
            for q in {q for q, _ in rides}:
                del moving[q]
        terms = [[terms[j]] + [came[i][j] for i in sorted(came)] for j in range(keeps)]
    for step in range(1, blocks):
        arrays.append(shift(leaving[step - 1], step))
        far_pieces.append((len(arrays) - 1, 0, rows))

    sums = pack("sum", [terms], nodes ** (-0.5), [arrays[piece[0]] for piece in far_pieces])[0].reshape(1, share, width)
    for bits in reversed(pairs):
        sums = jnp.concatenate([swap(sums, mask) for mask in masks(bits)])
    other = swap(sums, 1 << low)
    if aligned:
        grad_weight = kernel(
            functools.partial(place_kernel, order),
            "place",
            array((width, width), F32),
            (sums, other),
            traffic=8 * width * width,
        )
    else:
        places = jnp.array([order.index(i) for i in range(chunks)])[chunk_number(chunks) ^ jnp.arange(chunks)]
        grad_weight = jnp.concatenate([sums, other])[places].reshape(width, width)

    came = moving[0]
    used = sorted({piece[0] for _, piece in came} | {piece[0] for piece in far_pieces})
    grad_features = kernel(
        functools.partial(
            finish_kernel,
            [(distance, renumber(piece, used)) for distance, piece in came],
            [renumber(piece, used) for piece in far_pieces],
        ),
        "finish",
        array((rows, width), F32),
        (chosen, inner, *(arrays[i] for i in used)),
        scratch=(pltpu.VMEM((slots, width), F32),),
        flops=2 * work,
        traffic=4 * (3 * rows + slots) * width,
    )
    return (output, grad_features, grad_weight)


def solution(mesh):
    return jax.shard_map(
        body,
        mesh=mesh,
        in_specs=(
            P(("comm", "blk"), None),
            P(("comm", "blk"), None),
            P(),
            P(("comm", "blk"), None),
            P(("comm", "blk"), None),
            P(("comm", "blk"), None),
            P(("comm", "blk"), None),
            P(("comm", "blk"), None),
        ),
        out_specs=(P(("comm", "blk"), None), P(("comm", "blk"), None), P()),
        check_vma=False,
    )
```

```python
import functools
import math

import jax
import jax.numpy as jnp
from jax import lax
from jax.experimental import pallas as pl
from jax.experimental.pallas import tpu as pltpu
from jax.sharding import PartitionSpec as P

F32 = jnp.float32
BF16 = jnp.bfloat16
VMEM = pl.BlockSpec(memory_space=pltpu.VMEM)
HBM = pl.BlockSpec(memory_space=pltpu.HBM)


def split(value):
    high = value.astype(BF16)
    return high, (value - high.astype(F32)).astype(BF16)


def product(a, b, dims):
    return lax.dot_general(a, b, (dims, ((), ())), preferred_element_type=F32)


def dot3(a, b, dims=((1,), (0,))):
    (a_high, a_low), (b_high, b_low) = a, b
    left = jnp.concatenate([a_low, a_high, a_high], axis=dims[0][0])
    right = jnp.concatenate([b_high, b_low, b_high], axis=dims[1][0])
    return product(left, right, dims)


def dot_onehot(a, b, dims):
    left = jnp.concatenate([a, a], axis=dims[0][0])
    return product(left, jnp.concatenate([b[1], b[0]], axis=dims[1][0]), dims)


def tree(terms):
    while len(terms) > 1:
        terms = [terms[i] + terms[i + 1] for i in range(0, len(terms), 2)]
    return terms[0]


def send_matrix(counts, index, rows):
    groups, slots = counts.shape[1], index.shape[1]
    per_peer = slots // groups
    lane = lax.broadcasted_iota(jnp.int32, (groups, slots), 1)
    first = lax.broadcasted_iota(jnp.int32, (groups, slots), 0) * per_peer
    of_peer = ((lane >= first) & (lane < first + per_peer)).astype(F32)
    limit = jnp.dot(counts.astype(F32), of_peer, preferred_element_type=F32)
    place = lax.broadcasted_iota(jnp.int32, (1, slots), 1) % per_peer
    chosen = jnp.where(place.astype(F32) < limit, index, -1)
    return (lax.broadcasted_iota(jnp.int32, (rows, slots), 0) == chosen).astype(F32).astype(BF16)


def gather_kernel(
    count_hbm, index_hbm, features_hbm, own_ref, give_ref, chosen_ref, count_ref, index_ref, features_ref, rows_ref, sems
):
    pairs = ((count_hbm, count_ref), (index_hbm, index_ref), (features_hbm, features_ref))
    copies = [pltpu.make_async_copy(source, target, sems.at[i]) for i, (source, target) in enumerate(pairs)]
    for copy in copies:
        copy.start()
    copies[0].wait()
    copies[1].wait()
    chosen = send_matrix(count_ref[...], index_ref[...], features_ref.shape[0])
    chosen_ref[...] = chosen
    copies[2].wait()
    rows_ref[...] = dot_onehot(chosen, split(features_ref[...]), ((0,), (0,)))
    me = lax.axis_index("comm")
    chips, per_peer = own_ref.shape[:2]
    for mask in range(chips):
        for k, out_ref in enumerate((own_ref, give_ref)):
            start = lax.bitwise_xor(me, 2 * mask + (k ^ (mask > 0))) * per_peer
            out_ref[mask] = rows_ref[pl.ds(pl.multiple_of(start, per_peer), per_peer), :]


def prepare_kernel(
    near_ref, far_ref, tiles_ref, weight_ref, target_ref, edge_ref,
    local_ref, cross_ref, tiles_out, weight_out,
):
    rows = near_ref.shape[0]
    blocks = far_ref.shape[0] + 1
    slots = target_ref.shape[1]
    me = lax.axis_index("blk")

    total = None
    for step in range(blocks):
        start = lax.rem(me + step, blocks) * rows
        tile = split(tiles_ref[:, pl.ds(pl.multiple_of(start, rows), rows)])
        tiles_out[step, 0], tiles_out[step, 1] = tile
        term = dot3(tile, split(near_ref[...] if step == 0 else far_ref[step - 1]))
        total = term if total is None else total + term
    local_ref[...] = total
    hit = lax.broadcasted_iota(jnp.int32, (rows, slots), 0) == target_ref[...]
    cross_ref[0], cross_ref[1] = split(jnp.where(hit, edge_ref[...], 0.0))
    weight_out[0], weight_out[1] = split(weight_ref[...])


def chunk_number(chunks):
    blocks = lax.axis_size("blk")
    number = lax.axis_index("comm") * blocks + lax.axis_index("blk")
    outer = lax.div(number, chunks)
    crossed = lax.rem(outer + lax.div(outer, 2), 2) * blocks
    return lax.bitwise_xor(lax.rem(number, chunks), crossed)


def layer_kernel(
    order, parities, arrival, local_ref, cross_ref, weight_ref, cotangent_ref, own_ref, got_ref, *refs
):
    chips, per_peer = own_ref.shape[:2]
    arrived_refs, refs = refs[: chips - 1], refs[chips - 1 :]
    out_ref, spread_ref, keep_ref, give_ref, *partial_refs, slots_ref, terms_ref = refs
    peer = lax.axis_index("comm")
    for mask in range(chips):
        for k in range(2):
            start = lax.bitwise_xor(peer, 2 * mask + (k ^ (mask > 0))) * per_peer
            block = arrived_refs[arrival.index(mask - 1)][k] if mask else (got_ref if k else own_ref)[0]
            slots_ref[pl.ds(pl.multiple_of(start, per_peer), per_peer), :] = block
    cross = cross_ref[0], cross_ref[1]
    weight = weight_ref[0], weight_ref[1]

    aggregated = split(local_ref[...] + dot3(cross, split(slots_ref[...])))
    pre = dot3(aggregated, weight)
    cdf = 0.5 * (1.0 + lax.erf(pre * math.sqrt(0.5)))
    density = jnp.exp(-0.5 * pre * pre) * (1.0 / math.sqrt(2.0 * math.pi))
    grad_pre = split(cotangent_ref[...] * (cdf + pre * density))
    out_ref[...] = pre * cdf
    terms_ref[...] = dot3(aggregated, grad_pre, ((0,), (0,)))
    spread = split(dot3(grad_pre, weight, ((1,), (1,))))
    spread_ref[0], spread_ref[1] = spread
    slots_ref[...] = dot3(cross, spread, ((0,), (0,)))

    half = 0
    if partial_refs:
        partial_refs[0][...] = terms_ref[...]
    else:
        half = terms_ref.shape[0] // 2
        share = terms_ref.shape[0] // len(order)
        me = chunk_number(len(order))
        for place, relative in enumerate(order):
            start = lax.bitwise_xor(me, relative) * share
            chunk = terms_ref[pl.ds(pl.multiple_of(start, share), share), :]
            target_ref = keep_ref if place < len(order) // 2 else give_ref
            target_ref[pl.ds(place * share % half, share), :] = chunk
    for mask in range(chips):
        for k, target_ref in enumerate((keep_ref, give_ref)):
            start = lax.bitwise_xor(peer, 2 * mask + (k ^ parities[mask])) * per_peer
            block = slots_ref[pl.ds(pl.multiple_of(start, per_peer), per_peer), :]
            target_ref[pl.ds(half + mask * per_peer, per_peer), :] = block


def place_kernel(order, mine_ref, other_ref, out_ref):
    half, share = mine_ref.shape[:2]
    me = chunk_number(len(order))
    for i, relative in enumerate(order):
        start = lax.bitwise_xor(me, relative) * share
        out_ref[pl.ds(pl.multiple_of(start, share), share), :] = mine_ref[i] if i < half else other_ref[i - half]


def inner_kernel(tiles_ref, spread_ref, value_ref, near_ref, far_ref, out_ref):
    spread = spread_ref[0], spread_ref[1]
    for step in range(far_ref.shape[0]):
        far_ref[step] = dot3((tiles_ref[step + 1, 0], tiles_ref[step + 1, 1]), spread, ((0,), (0,)))
    near_ref[...] = dot3((tiles_ref[0, 0], tiles_ref[0, 1]), spread, ((0,), (0,)))
    out_ref[...] = value_ref[...]


def value_of(piece, refs):
    if isinstance(piece, list):
        return tree([value_of(term, refs) for term in piece])
    source, first, rows = piece
    return refs[source][first : first + rows, :]


def rows_of(piece):
    return rows_of(piece[0]) if isinstance(piece, list) else piece[2]


def leaves(piece):
    return [leaf for term in piece for leaf in leaves(term)] if isinstance(piece, list) else [piece]


def renumber(piece, used):
    if isinstance(piece, list):
        return [renumber(term, used) for term in piece]
    return (used.index(piece[0]), *piece[1:])


def pack_kernel(layout, scale, count, *refs):
    for pieces, out_ref in zip(layout, refs[count:]):
        first = 0
        for piece in pieces:
            rows = rows_of(piece)
            value = value_of(piece, refs)
            out_ref[first : first + rows, :] = value if scale is None else value * scale
            first += rows


def finish_kernel(blocks, far, chosen_ref, near_ref, *refs):
    *refs, grad_ref, slots_ref = refs
    peer = lax.axis_index("comm")
    for distance, piece in blocks:
        rows = piece[2]
        start = lax.bitwise_xor(peer, distance) * rows
        slots_ref[pl.ds(pl.multiple_of(start, rows), rows), :] = value_of(piece, refs)
    total = near_ref[...]
    for piece in far:
        total += value_of(piece, refs)
    grad_ref[...] = total + dot_onehot(chosen_ref[...], split(slots_ref[...]), ((1,), (0,)))


def kernel(body, name, out, operands, spec=VMEM, scratch=(), flops=0, traffic=0, after=()):
    count = len(operands)
    if spec is HBM:
        operands = [pltpu.with_memory_space_constraint(x, pltpu.HBM) for x in operands]
    return pl.pallas_call(
        lambda *refs: body(*refs[:count], *refs[count + len(after) :]),
        out_shape=out,
        in_specs=[spec] * count + [pl.BlockSpec(memory_space=pl.ANY)] * len(after),
        out_specs=jax.tree.map(lambda _: VMEM, out),
        scratch_shapes=list(scratch),
        compiler_params=pltpu.CompilerParams(vmem_limit_bytes=16 * 1024 * 1024),
        cost_estimate=pl.CostEstimate(flops=flops, bytes_accessed=traffic, transcendentals=0),
        name=name,
    )(*operands, *after)


def body(features, tiles, weight, cotangent, send_count, send_index, cross_dst, cross_weight):
    rows, width = features.shape
    groups = lax.axis_size("comm")
    blocks = lax.axis_size("blk")
    slots = send_index.shape[1]
    per_peer = slots // groups
    nodes = rows * groups * blocks
    array = jax.ShapeDtypeStruct
    work = 2 * rows * slots * width

    def shift(value, step):
        pairs = [(i, (i + step) % blocks) for i in range(blocks)]
        return lax.ppermute(value, "blk", pairs)

    def exchange(value):
        return lax.all_to_all(value, "comm", split_axis=0, concat_axis=0, tiled=True)

    both = ("comm", "blk")
    devices = groups * blocks
    outer = min(4, groups // 2)
    chunks = devices // outer
    share = width // chunks
    low, high = blocks.bit_length() - 1, chunks.bit_length() - 1
    others = list(range(low)) + list(range(low + 1, high))
    pairs = [others[i : i + 2] for i in range(0, len(others), 2)]

    core = 1 << low
    outer_bits = list(range(high, devices.bit_length() - 1))

    def masks(bits, straight=()):
        plain = [sum((i >> j & 1) << bit for j, bit in enumerate(bits)) for i in range(1 << len(bits))]
        if bits is outer_bits:
            return [mask ^ core * (i.bit_count() % 2) for i, mask in enumerate(plain)]
        return [mask if mask in (0, core) or mask in straight else mask ^ core for mask in plain]

    def order_of(straight=()):
        order = [0]
        for bits in reversed([[low]] + pairs):
            order = [mask ^ place for mask in masks(bits, straight) for place in order]
        return order

    straight = (1,) if blocks == 2 else ()
    order, gather_order = order_of(straight), order_of()
    way_bits = [sum(1 << bit - low - 1 for bit in bits if bit > low) for bits in pairs]
    parities = [
        (sum(bool(chip & bits) for bits in way_bits) + (chip >> high - low - 1).bit_count()) % 2
        for chip in range(groups // 2)
    ]

    def swap(value, mask):
        return lax.ppermute(value, both, [(i, i ^ mask) for i in range(devices)]) if mask else value

    far = jnp.stack([shift(features, -step) for step in range(1, blocks)])
    own, give, chosen = kernel(
        gather_kernel,
        "gather",
        (
            array((groups // 2, per_peer, width), F32),
            array((groups // 2, per_peer, width), F32),
            array((rows, slots), BF16),
        ),
        (send_count, send_index, features),
        spec=HBM,
        scratch=(
            pltpu.VMEM(send_count.shape, jnp.int32),
            pltpu.VMEM(send_index.shape, jnp.int32),
            pltpu.VMEM(features.shape, F32),
            pltpu.VMEM((slots, width), F32),
            pltpu.SemaphoreType.DMA((3,)),
        ),
        flops=work,
        traffic=4 * (rows + slots) * width,
    )
    got = swap(give, 1 << low)
    packed = jnp.stack([own, got], axis=1)
    arrived = [swap(packed[mask], 2 * mask + 1 << low) for mask in range(1, groups // 2)]
    arrival = list(range(groups // 2 - 1))
    two, three = groups // 4 - 1, 3 * groups // 8 - 1
    arrival = [i for i in arrival if i not in (two, three)] + [three, two]
    local, cross, tile_parts, weight_parts = kernel(
        prepare_kernel,
        "prepare",
        (
            array((rows, width), F32),
            array((2, rows, slots), BF16),
            array((blocks, 2, rows, rows), BF16),
            array((2, width, width), BF16),
        ),
        (features, far, tiles, weight, cross_dst, cross_weight),
        flops=3 * work,
        traffic=4 * (4 * rows + width) * width,
    )
    aligned = share % 8 == 0
    half = width // 2
    held = array((slots // 2 + (half if aligned else 0), width), F32)
    value, spread, keep, give, *partial = kernel(
        functools.partial(layer_kernel, order, parities, arrival),
        "layer",
        (array((rows, width), F32), array((2, rows, width), BF16), held, held)
        + (() if aligned else (array((width, width), F32),)),
        (local, cross, weight_parts, cotangent, own, got, *(arrived[i] for i in arrival)),
        scratch=(pltpu.VMEM((slots, width), F32), pltpu.VMEM((width, width), F32)),
        flops=15 * work,
        traffic=4 * (4 * rows + 2 * slots) * width,
    )
    if not aligned:
        ordered = partial[0].reshape(chunks, share, width)[chunk_number(chunks) ^ jnp.array(order)]
        keep = jnp.concatenate([ordered[: chunks // 2].reshape(half, width), keep])
        give = jnp.concatenate([ordered[chunks // 2 :].reshape(half, width), give])
    inner, leaving, output = kernel(
        inner_kernel,
        "inner",
        (array((rows, width), F32), array((blocks - 1, rows, width), F32), array((rows, width), F32)),
        (tile_parts, spread, value),
        flops=3 * work,
        traffic=4 * 6 * rows * width,
    )

    arrays = [keep, give, swap(give, 1 << low)]
    terms = [[(0, i * share, share), (2, i * share, share)] for i in range(chunks // 2)]
    moving = {
        2 * m + parities[m]: [(k, (2 * k, half + m * per_peer, per_peer)) for k in range(2)]
        for m in range(groups // 2)
    }
    far_pieces = []

    def pack(name, layout, scale=None):
        used = sorted({leaf[0] for pieces in layout for leaf in leaves(pieces)})
        layout = [[renumber(piece, used) for piece in pieces] for pieces in layout]
        out = tuple(array((sum(map(rows_of, pieces)), width), F32) for pieces in layout)
        operands = [arrays[i] for i in used]
        traffic = 8 * width * sum(o.shape[0] for o in out)
        return kernel(functools.partial(pack_kernel, layout, scale, len(used)), name, out, operands, traffic=traffic)

    for bits in pairs + [outer_bits]:
        last = bits is outer_bits
        keeps = len(terms) if last else len(terms) >> len(bits)
        layout, riders = [], []
        partners = list(enumerate(masks(bits, straight)))[:0:-1]
        if last:
            partners.sort(key=lambda partner: partner[0] != 2)
        for i, mask in partners:
            pieces = list(terms) if last else terms[i * keeps : (i + 1) * keeps]
            way, across = mask >> low, mask & (core - 1)
            all_ways = sum(1 << bit for bit in bits) >> low
            going = [q for q in sorted(moving) if not across and q & all_ways == way & all_ways]
            riders.append([(q, come) for q in going for come, _ in moving[q]])
            pieces += [piece for q in going for _, piece in moving[q]]
            if blocks == 2 and mask == 1:
                arrays.append(leaving[0])
                pieces.append((len(arrays) - 1, 0, rows))
            layout.append(pieces)
        sent = pack("pack", layout)
        came = {}
        for (i, mask), value, rides in zip(partners, sent, riders):
            arrays.append(swap(value, mask))
            number, first = len(arrays) - 1, 0
            came[i] = [(number, j * share, share) for j in range(keeps)]
            first = keeps * share
            for q, come in rides:
                way = mask >> low
                moving.setdefault(q ^ way, []).append((come ^ way, (number, first, per_peer)))
                first += per_peer
            if blocks == 2 and mask == 1:
                far_pieces.append((number, first, rows))
            for q in {q for q, _ in rides}:
                del moving[q]
        terms = [[terms[j]] + [came[i][j] for i in sorted(came)] for j in range(keeps)]
    if blocks > 2:
        for step in range(1, blocks):
            arrays.append(shift(leaving[step - 1], step))
            far_pieces.append((len(arrays) - 1, 0, rows))

    sums = pack("sum", [terms], nodes ** (-0.5))[0].reshape(1, share, width)
    for bits in reversed(pairs):
        sums = jnp.concatenate([swap(sums, mask) for mask in masks(bits)])
    other = swap(sums, 1 << low)
    if aligned:
        grad_weight = kernel(
            functools.partial(place_kernel, gather_order),
            "place",
            array((width, width), F32),
            (sums, other),
            traffic=8 * width * width,
        )
    else:
        places = jnp.array([gather_order.index(i) for i in range(chunks)])[chunk_number(chunks) ^ jnp.arange(chunks)]
        grad_weight = jnp.concatenate([sums, other])[places].reshape(width, width)

    came = moving[0]
    used = sorted({piece[0] for _, piece in came} | {piece[0] for piece in far_pieces})
    grad_features = kernel(
        functools.partial(
            finish_kernel,
            [(distance, renumber(piece, used)) for distance, piece in came],
            [renumber(piece, used) for piece in far_pieces],
        ),
        "finish",
        array((rows, width), F32),
        (chosen, inner, *(arrays[i] for i in used)),
        scratch=(pltpu.VMEM((slots, width), F32),),
        flops=2 * work,
        traffic=4 * (3 * rows + slots) * width,
    )
    return (output, grad_features, grad_weight)


def solution(mesh):
    return jax.shard_map(
        body,
        mesh=mesh,
        in_specs=(
            P(("comm", "blk"), None),
            P(("comm", "blk"), None),
            P(),
            P(("comm", "blk"), None),
            P(("comm", "blk"), None),
            P(("comm", "blk"), None),
            P(("comm", "blk"), None),
            P(("comm", "blk"), None),
        ),
        out_specs=(P(("comm", "blk"), None), P(("comm", "blk"), None), P()),
        check_vma=False,
    )
```
